128 devices in a mesh: fsdp: 64 (over y_lo, x, z, core), tp: 2 (over y_hi).
Axes of the slice: x: 4, y: 4 (y_hi: 2, y_lo: 2; y = y_hi * 2 + y_lo), z: 4, core: 2. Of those that a mesh axis runs over, the one named last changes fastest.
Arguments:
- activations: bfloat16 [25216, 768], P(('fsdp', 'tp')), may hold values from -24 to 24
- attn_gain: bfloat16 [2, 768], P(None, 'fsdp'), may hold values from 0.25 to 1.75
- qkv_weight: bfloat16 [2, 3, 768, 768], P(None, None, 'fsdp', 'tp'), may hold values from -0.21875 to 0.21875
- out_weight: bfloat16 [2, 768, 768], P(None, 'tp', 'fsdp'), may hold values from -0.875 to 0.875
- ffn_gain: bfloat16 [2, 768], P(None, 'fsdp'), may hold values from 0.25 to 1.75
- mlp_up: bfloat16 [768, 3072], P('fsdp', 'tp'), may hold values from -0.21875 to 0.21875
- mlp_down: bfloat16 [3072, 768], P('tp', 'fsdp'), may hold values from -0.109375 to 0.109375
- router: bfloat16 [768, 4], P('fsdp'), may hold values from -0.15625 to 0.15625
- expert_up: bfloat16 [4, 768, 3072], P(None, 'fsdp', 'tp'), may hold values from -0.21875 to 0.21875
- expert_down: bfloat16 [4, 3072, 768], P(None, 'tp', 'fsdp'), may hold values from -0.21875 to 0.21875
- routes: int32 [25216, 2], P('fsdp'), may hold values from 0 to 3, all different within a row; in each aligned block of 394 rows (0 to 393, 394 to 787, ...) at most 256 rows name the same one
- cotangent: bfloat16 [25216, 768], P(('fsdp', 'tp')), may hold values from -24 to 24
Outputs:
- result: bfloat16 [25216, 768], P(('fsdp', 'tp'))
- input_grad: float32 [25216, 768], P(('fsdp', 'tp'))
- attn_gain_grad: float32 [2, 768], P(None, 'fsdp')
- qkv_grad: float32 [2, 3, 768, 768], P(None, None, 'fsdp', 'tp')
- out_grad: float32 [2, 768, 768], P(None, 'tp', 'fsdp')
- ffn_gain_grad: float32 [2, 768], P(None, 'fsdp')
- mlp_up_grad: float32 [768, 3072], P('fsdp', 'tp')
- mlp_down_grad: float32 [3072, 768], P('tp', 'fsdp')
- router_grad: float32 [768, 4], P('fsdp')
- expert_up_grad: float32 [4, 768, 3072], P(None, 'fsdp', 'tp')
- expert_down_grad: float32 [4, 3072, 768], P(None, 'tp', 'fsdp')
The draws below stay inside these ranges and needn't reach their ends.
Inputs may be any that keep to these rules, and one draw needn't show every extreme that they name: `routes`: each row names 2 different experts. In each aligned block of 394 rows (the images of one index of fsdp) no expert is named by more than 256 rows, a bound that some block reaches.
All inputs are finite; a program needn't handle non-finite values.
Results may differ from the reference program's by a relative error of at most 0.025.
Values may be sent and summed in bfloat16 or wider, within the bound.
A program may use at most 320 MiB of HBM per device.

```python
import math
import jax
import jax.numpy as jnp
import numpy as np
from jax import lax

D = 768
HEADS = 12
HEAD = 64
FF = 3072
SEQ = 197
EXPERTS = 4
TOP = 2
ROWS = 394
CAP = 256
TOKENS = 25216
N_FSDP = 64


def strengthened(drawn, stream_key, source, target, shards_of, factor):
    owner, partner = [(jnp.arange(drawn.shape[dim]) // (drawn.shape[dim] // shards_of)).reshape([-1 if axis == dim else 1 for axis in range(drawn.ndim)]) for dim in (source, target)]
    chosen = jax.random.permutation(stream_key, shards_of)[partner]
    strong = (owner == chosen) | (owner == (partner + shards_of // 2) % shards_of)
    return jnp.where(strong, factor * drawn, drawn)


def block_levels(key, dims, shards, low, largest):
    level, own = 1.0, jax.random.fold_in(key, 6)
    for position, blocks in shards:
        steps = jnp.exp(jax.random.uniform(jax.random.fold_in(own, position), (blocks,), jnp.float32, low / len(shards), largest / len(shards)))
        level = level * jnp.repeat(steps, dims[position] // blocks).reshape([-1 if axis == position else 1 for axis in range(len(dims))])
    return level


def routed_block(key, own, number, rows, number_of, top, limit, skew):
    sequence = jax.random.permutation(key, number_of)
    heavy_load, ordinary = load_shares(number_of, rows * top, limit, skew, True), load_shares(number_of, rows * top, limit, skew, False)
    places = jnp.arange(number_of)

    def named(sizes, turn):
        used = int((sizes > 0).sum())
        fixed = max(1, used // 4)
        shifted = fixed + (places - fixed + turn * (used - fixed)) % max(1, number_of - fixed)
        return jnp.zeros((number_of,), jnp.int32).at[sequence[jnp.where(places < fixed, places, shifted)]].set(jnp.asarray(sizes, jnp.int32))

    sizes = jnp.where(number % 4 == 0, named(heavy_load, number // 4), named(ordinary, number - number // 4 - 1))
    mixed = jax.random.permutation(jax.random.fold_in(own, 3), number_of)
    source_of, taker = mixed[0:number_of // 2 * 2:2], mixed[1:number_of // 2 * 2:2]
    margin = jnp.minimum(sizes[source_of] - 1, limit - sizes[taker]) // 2
    margin = jnp.where((source_of == sequence[0]) | (taker == sequence[0]) | (sizes[taker] == 0), 0, jnp.maximum(margin, 0))
    shifted = jax.random.randint(jax.random.fold_in(own, 4), (number_of // 2,), 0, 1 << 20) % (margin + 1)
    sizes = sizes.at[source_of].add(-shifted).at[taker].add(shifted)
    members = jnp.searchsorted(jnp.cumsum(sizes), jnp.arange(rows * top), side="right").astype(jnp.int32)
    table = members.reshape(top, rows).T
    table = table[jax.random.permutation(jax.random.fold_in(own, 1), rows)]
    turn = jax.random.randint(jax.random.fold_in(own, 2), (rows, 1), 0, top)
    return jnp.take_along_axis(table, (jnp.arange(top)[None, :] + turn) % top, axis=1)


def load_shares(amount, total, limit, skew, full):
    weights = [(1 << 20) // math.isqrt(grade ** skew) + 1 for grade in range(1, amount + 1)]
    largest = limit if full else min(limit, max(-(-total // amount), total * weights[0] // sum(weights)))
    least = 1 if total - largest >= amount - 1 else 0
    given, rest = [largest] + [least] * (amount - 1), total - largest - least * (amount - 1)
    while rest > 0:
        candidates = [i for i in range(1, amount) if given[i] < largest] or [i for i in range(1, amount) if given[i] < limit]
        mass, left = sum([weights[i] for i in candidates]), rest
        for i in candidates:
            addition = min(limit - given[i], max(1, left * weights[i] // mass), rest)
            given[i] = given[i] + addition
            rest = rest - addition
    return np.array(given)


def normal_values(rng, shape, scale, most, split=(), kind=jnp.bfloat16):
    factor_of = block_levels(rng, shape, split, -0.22, 0.18) if split else 1.0
    values = jax.random.normal(rng, shape, jnp.float32) * scale * factor_of
    return jnp.minimum(jnp.maximum(values, -most), most).astype(kind)


def bell_draw_with(own_key, dims, scale, reach, pieces, heavy, kind=jnp.bfloat16):
    array = scale * jax.random.normal(own_key, dims, jnp.float32)
    if pieces:
        array = array * block_levels(own_key, dims, pieces, -0.22, 0.18)
    return jnp.clip(strengthened(array, jax.random.fold_in(own_key, 3), *heavy), -reach, reach).astype(kind)


def setup_inputs(seed: int = 0) -> dict:
    keys = jax.random.split(jax.random.key(seed), 13)
    activations = bell_draw_with(keys[0], (TOKENS, D), 1.0, 24.0, ((0, 128),), (0, 1, 128, 5.5))
    attn_gain = jnp.clip(1.0 + 0.15 * jax.random.normal(keys[1], (2, D), jnp.float32), 0.25, 1.75).astype(jnp.bfloat16)
    qkv_weight = normal_values(keys[2], (2, 3, D, D), D ** -0.5, 0.21875, ((2, 64), (3, 2)))
    out_weight = normal_values(keys[3], (2, D, D), (D // 16) ** -0.5, 0.875, ((1, 2), (2, 64)))
    ffn_gain = jnp.clip(1.0 + 0.15 * jax.random.normal(keys[4], (2, D), jnp.float32), 0.25, 1.75).astype(jnp.bfloat16)
    mlp_up = normal_values(keys[5], (D, FF), D ** -0.5, 0.21875, ((0, 64), (1, 2)))
    mlp_down = normal_values(keys[6], (FF, D), FF ** -0.5, 0.109375, ((0, 2), (1, 64)))
    router = normal_values(keys[7], (D, EXPERTS), (2 * D) ** -0.5, 0.15625, ((0, 64),))
    expert_up = normal_values(keys[8], (EXPERTS, D, FF), D ** -0.5, 0.21875, ((1, 64), (2, 2)))
    expert_down = normal_values(keys[9], (EXPERTS, FF, D), (FF // 4) ** -0.5, 0.21875, ((1, 2), (2, 64)))
    routes_keys = jax.random.split(jax.random.fold_in(keys[10], 1), TOKENS // ROWS)
    routes_turns = jax.random.permutation(jax.random.fold_in(keys[10], 3), TOKENS // ROWS)
    routes = jax.vmap(lambda own, number: routed_block(jax.random.fold_in(keys[10], 2), own, number, ROWS, EXPERTS, TOP, CAP, 1))(routes_keys, routes_turns).reshape((TOKENS, TOP))
    cotangent = bell_draw_with(keys[11], (TOKENS, D), 1.0, 24.0, ((0, 128),), (0, 1, 128, 5.5))
    return dict(activations=activations, attn_gain=attn_gain, qkv_weight=qkv_weight, out_weight=out_weight, ffn_gain=ffn_gain, mlp_up=mlp_up, mlp_down=mlp_down, router=router, expert_up=expert_up, expert_down=expert_down, routes=routes, cotangent=cotangent)


epsilon = 1e-06
precise = lax.Precision.HIGHEST

@jax.custom_vjp
def low(v):
    return lax.optimization_barrier(v.astype(jnp.bfloat16)).astype(jnp.float32)

@jax.custom_vjp
def low_back(v):
    return v

def low_keep(v):
    return (low(v), None)

def low_pass(kept, grad):
    return (grad,)

def back_keep(v):
    return (v, None)

def back_low(kept, grad):
    return (low(grad),)
low.defvjp(low_keep, low_pass)
low_back.defvjp(back_keep, back_low)

def both_ways(value_in):
    return low(low_back(value_in))

def product(left, right):
    return jnp.dot(left, right, precision=precise, preferred_element_type=jnp.float32)

def normed(values, norm_gain):
    centre = values - lax.optimization_barrier(jnp.mean(values, axis=-1, keepdims=True))
    spread = lax.optimization_barrier(jnp.mean(centre * centre, axis=-1, keepdims=True))
    return centre * lax.rsqrt(spread + epsilon) * norm_gain

def attention(residual, norm_gain, qkv_matrix, out_matrix):
    inputs = low(normed(residual, norm_gain))
    token_count = residual.shape[0]
    shaped = (token_count // SEQ, SEQ, HEADS, HEAD)
    query_vectors = both_ways(product(inputs, qkv_matrix[0])).reshape(shaped)
    key_vectors = both_ways(product(inputs, qkv_matrix[1])).reshape(shaped)
    value_vectors = both_ways(product(inputs, qkv_matrix[2])).reshape(shaped)
    raw_scores = jnp.einsum('ishd,ithd->ihst', query_vectors, key_vectors, precision=precise)
    scores = low_back(raw_scores * HEAD ** (-0.5))
    attn_probs = jax.nn.softmax(scores, axis=-1)
    mixed_heads = jnp.einsum('ihst,ithd->ishd', low(attn_probs), value_vectors, precision=precise)
    mixed_heads = both_ways(mixed_heads.reshape(token_count, HEADS * HEAD))
    return low_back(product(mixed_heads, out_matrix))

def dense(residual, norm_gain, up_matrix, down_matrix):
    inputs = low(normed(residual, norm_gain))
    hidden_pre = low_back(product(inputs, up_matrix))
    activated = low(jax.nn.gelu(hidden_pre, approximate=False))
    return low_back(product(activated, down_matrix))

def experts_branch(residual, norm_gain, router_matrix, up_stack, down_stack, route_block):
    inputs = low(normed(residual, norm_gain))
    router_probs = jax.nn.softmax(product(inputs, router_matrix), axis=-1)
    labels = jnp.arange(EXPERTS, dtype=jnp.int32)
    chosen = lax.optimization_barrier(jnp.sum((route_block[:, :, None] == labels[None, None, :]).astype(jnp.float32), axis=1))
    combine = router_probs * chosen
    mixture = jnp.zeros_like(residual)
    for expert in range(EXPERTS):
        hidden_pre = low_back(product(inputs, up_stack[expert]))
        activated = low(jax.nn.gelu(hidden_pre, approximate=False))
        expert_out = low_back(product(activated, down_stack[expert]))
        mixture = mixture + combine[:, expert:expert + 1] * expert_out
    return low_back(mixture)

def forward(weights, residual, route_block):
    attn_gain, qkv_weight, out_weight, ffn_gain, mlp_up, mlp_down, router, expert_up, expert_down = weights
    residual = residual + attention(residual, attn_gain[0], qkv_weight[0], out_weight[0])
    residual = residual + dense(residual, ffn_gain[0], mlp_up, mlp_down)
    residual = residual + attention(residual, attn_gain[1], qkv_weight[1], out_weight[1])
    residual = residual + experts_branch(residual, ffn_gain[1], router, expert_up, expert_down, route_block)
    return residual

def reference(activations, attn_gain, qkv_weight, out_weight, ffn_gain, mlp_up, mlp_down, router, expert_up, expert_down, routes, cotangent):
    weights = (attn_gain, qkv_weight, out_weight, ffn_gain, mlp_up, mlp_down, router, expert_up, expert_down)
    weights = jax.tree.map(lambda member: member.astype(jnp.float32), weights)
    token_blocks = activations.astype(jnp.float32).reshape(N_FSDP, ROWS, D)
    route_blocks = routes.reshape(N_FSDP, ROWS, TOP)
    grad_blocks = cotangent.astype(jnp.float32).reshape(N_FSDP, ROWS, D)

    def step(totals, block):
        token_block, route_block, grad_block = block

        def run(weight_set, token_set):
            return forward(weight_set, token_set, route_block)
        output, pullback = jax.vjp(run, weights, token_block)
        weight_grads, token_grads = pullback(grad_block)
        totals = jax.tree.map(lambda first, second: first + second, totals, weight_grads)
        return (totals, (output, token_grads))
    zero_grads = jax.tree.map(jnp.zeros_like, weights)
    totals, (outputs, token_grads) = lax.scan(step, zero_grads, (token_blocks, route_blocks, grad_blocks))
    result = outputs.reshape(TOKENS, D).astype(jnp.bfloat16)
    input_grad = token_grads.reshape(TOKENS, D)
    return (result, input_grad, totals[0], totals[1], totals[2], totals[3], totals[4], totals[5], totals[6], totals[7], totals[8])
```

```python
import functools
import itertools

import jax
import jax.numpy as jnp
from jax import lax
from jax.experimental import pallas as pl
from jax.experimental.pallas import tpu as pltpu
from jax.sharding import PartitionSpec as P

HEAD = 64
SEQ = 197
D = 768
HALF = 1536
SMALL = 128
WIDE = HALF + SMALL
MESH = pl.DeviceIdType.MESH
GROUPS = [[4 * k + j for j in range(4)] for k in range(16)]

epsilon = 1e-06
precise = lax.Precision.HIGHEST

ORDERS = (("x", "y", "z"), ("y", "z", "x"), ("z", "x", "y"))
WIDTHS = (WIDE, HALF, HALF)


def to_low(values):
    return values.astype(jnp.bfloat16)


def coordinates():
    f, t = lax.axis_index("fsdp"), lax.axis_index("tp")
    return {
        "x": lax.rem(lax.div(f, 8), 4),
        "y": 2 * t + lax.div(f, 32),
        "z": lax.rem(lax.div(f, 2), 4),
        "c": lax.rem(f, 2),
    }


def device_at(place):
    y = place["y"]
    f = ((lax.rem(y, 2) * 4 + place["x"]) * 4 + place["z"]) * 2 + place["c"]
    return (f, lax.div(y, 2))


def moved(place, axis, steps):
    return {**place, axis: lax.rem(place[axis] + steps + 4, 4)}


def greet(place):
    others = [device_at(moved(place, a, s)) for a in "xyz" for s in (1, -1)]
    others.append(device_at({**place, "c": 1 - place["c"]}))
    barrier = pltpu.get_barrier_semaphore()
    for other in others:
        pl.semaphore_signal(barrier, inc=1, device_id=other, device_id_type=MESH)
    pl.semaphore_wait(barrier, len(others))


def cube(where, whole):
    every = slice(None)
    y = (every, every) if "y" in whole else (lax.div(where["y"], 2), lax.rem(where["y"], 2))
    z = (every, every) if "z" in whole else (lax.rem(where["z"], 2), lax.div(where["z"], 2))
    x = every if "x" in whole else where["x"]
    return (z[0], y[0], y[1], x, z[1])


def halves(width):
    first = (width // 256) * 128
    if width - first > first:
        first = width - first
    return (slice(0, first), slice(first, width))


def gather_kernel(*refs):
    n = len(WIDTHS)
    shards, wholes = refs[:n], refs[n : 2 * n]
    send_sem, recv_sem, send_pair, recv_pair, own_sem = refs[2 * n :]
    me = coordinates()
    sibling = {**me, "c": 1 - me["c"]}
    greet(me)

    def block(m, p, where, whole, cols=slice(None)):
        z_lo, t, y_lo, x, z_hi = cube(where, whole)
        return wholes[m].at[z_lo, me["c"], t, y_lo, x, z_hi, pl.ds(16 * p, 16), cols]

    pending = []
    pair_count = [0] * n

    def pair_send(src, dst, m):
        slot = pair_count[m]
        pair_count[m] += 1
        copy = pltpu.make_async_remote_copy(
            src_ref=src,
            dst_ref=dst,
            send_sem=send_pair.at[m, slot],
            recv_sem=recv_pair.at[m, slot],
            device_id=device_at(sibling),
            device_id_type=MESH,
        )
        copy.start()
        pending.append(copy)

    owns = []
    for m in range(n):
        z_lo, t, y_lo, x, z_hi = cube(me, ())
        mine = wholes[m].at[z_lo, me["c"], t, y_lo, x, z_hi]
        own = pltpu.make_async_copy(shards[m], mine, own_sem.at[m])
        own.start()
        owns.append(own)
    ici = []

    def ici_send(m, p, phase, kind, src, dst, target):
        copy = pltpu.make_async_remote_copy(
            src_ref=src,
            dst_ref=dst,
            send_sem=send_sem.at[m, p, phase, kind],
            recv_sem=recv_sem.at[m, p, phase, kind],
            device_id=device_at(target),
            device_id_type=MESH,
        )
        copy.start()
        ici.append(copy)
        return copy

    for phase in range(3):
        first = {}
        for m in range(n):
            for p in range(3):
                axis, done = ORDERS[p][phase], ORDERS[p][:phase]
                dst = block(m, p, me, done)
                src = shards[m].at[pl.ds(16 * p, 16)] if phase == 0 else dst
                first[m, p] = [
                    ici_send(m, p, phase, kind, src, dst, moved(me, axis, step))
                    for kind, step in ((0, 1), (1, -1))
                ]
            if phase == 0:
                z_lo, t, y_lo, x, z_hi = cube(me, ())
                pair_send(shards[m], wholes[m].at[z_lo, me["c"], t, y_lo, x, z_hi], m)
        second = {}
        for m in range(n):
            for p in range(3):
                axis, done = ORDERS[p][phase], ORDERS[p][:phase]
                cols = halves(WIDTHS[m])
                out = []
                for kind, step in ((0, 1), (1, -1)):
                    first[m, p][kind].wait_recv()
                    came = moved(me, axis, -step)
                    part = block(m, p, came, done, cols[kind])
                    out.append(ici_send(m, p, phase, 2 + kind, part, part, moved(me, axis, step)))
                second[m, p] = out
                for step in (1, -1):
                    part = block(m, p, moved(me, axis, -step), done)
                    pair_send(part, part, m)
        for m in range(n):
            for p in range(3):
                axis, done = ORDERS[p][phase], ORDERS[p][:phase]
                for kind in (0, 1):
                    second[m, p][kind].wait_recv()
                part = block(m, p, moved(me, axis, 2), done)
                pair_send(part, part, m)
        if phase == 0:
            for own in owns:
                own.wait()
    for copy in ici:
        copy.wait_send()
    for copy in pending:
        copy.wait()


def gather(shards):
    n = len(WIDTHS)
    dma = pltpu.SemaphoreType.DMA
    return pl.pallas_call(
        gather_kernel,
        out_shape=[
            jax.ShapeDtypeStruct((2, 2, 2, 2, 4, 2, 48, w), jnp.bfloat16) for w in WIDTHS
        ],
        in_specs=[pl.BlockSpec(memory_space=pl.ANY)] * n,
        out_specs=[pl.BlockSpec(memory_space=pl.ANY)] * n,
        scratch_shapes=[
            dma((n, 3, 3, 4)),
            dma((n, 3, 3, 4)),
            dma((n, 28)),
            dma((n, 28)),
            dma((n,)),
        ],
        compiler_params=pltpu.CompilerParams(collective_id=0, has_side_effects=True),
        name="gather_weights",
    )(*shards)


def lead_of(whole):
    dims = []
    if "z" in whole:
        dims.append(2)
    if "y" in whole:
        dims += [2, 2]
    if "x" in whole:
        dims.append(4)
    if "z" in whole:
        dims.append(2)
    return tuple(dims)


def split_index(i, dims):
    out = []
    for size in reversed(dims):
        out.append(lax.rem(i, size))
        i = lax.div(i, size)
    return tuple(reversed(out))


def with_index(where, whole, index):
    rest = list(index)
    full = list(cube(where, whole))
    for place, value in enumerate(full):
        if isinstance(value, slice):
            full[place] = rest.pop(0)
    return tuple(full)


RS_ORDERS = tuple(tuple(reversed(order)) for order in ORDERS)
SEQUENCE = (
    (0, 0), (1, 0), (0, 1), (2, 0), (1, 1), (0, 2), (2, 1), (0, 3), (1, 2), (0, 4), (1, 3),
    (2, 2), (0, 5), (1, 4), (2, 3), (0, 6), (1, 5), (2, 4), (1, 6), (2, 5), (2, 6),
)


def reduce_scratch():
    shapes = []
    for w in WIDTHS:
        shapes.append(pltpu.VMEM((2, 2, 2, 4, 2, 48, w), jnp.bfloat16))
        cols = halves(w)
        for p in range(3):
            for phase in range(3):
                lead = lead_of(RS_ORDERS[p][phase + 1 :])
                for part in cols:
                    shapes.append(
                        pltpu.VMEM((*lead, 16, part.stop - part.start), jnp.bfloat16)
                    )
                for _ in range(2):
                    shapes.append(pltpu.VMEM((*lead, 16, w), jnp.bfloat16))
    return shapes


def reduce_kernel(*refs):
    n = len(WIDTHS)
    grads = [refs[4 * m : 4 * m + 4] for m in range(n)]
    refs = refs[4 * n :]
    sums, refs = refs[:n], refs[n:]
    landing, refs = refs[:n], refs[n:]
    held, boxes = [], {}
    for m in range(n):
        held.append(refs[0])
        refs = refs[1:]
        for p in range(3):
            for phase in range(3):
                boxes[m, p, phase] = refs[:4]
                refs = refs[4:]
    stage, send_sem, recv_sem, send_pair, recv_pair, own_sem, stage_sem = refs
    me = coordinates()
    sibling = {**me, "c": 1 - me["c"]}
    greet(me)

    def own_copy(m, z_lo, src):
        return pltpu.make_async_copy(src, held[m].at[z_lo], own_sem.at[m, z_lo])

    def pair_copy(m, z_lo, src):
        return pltpu.make_async_remote_copy(
            src_ref=src,
            dst_ref=landing[m].at[z_lo],
            send_sem=send_pair.at[m, z_lo],
            recv_sem=recv_pair.at[m, z_lo],
            device_id=device_at(sibling),
            device_id_type=MESH,
        )

    for m in range(n):
        for z_lo in range(2):
            for c in range(2):

                @pl.when(me["c"] == c)
                def _():
                    pair_copy(m, z_lo, grads[m][2 * z_lo + 1 - c]).start()
                    own_copy(m, z_lo, grads[m][2 * z_lo + c]).start()

    def stage_copy(m, i, slot):
        z_lo, t, y_lo, x = split_index(i, (2, 2, 2, 4))
        return pltpu.make_async_copy(
            landing[m].at[z_lo, t, y_lo, x],
            stage.at[slot, :, :, pl.ds(0, WIDTHS[m])],
            stage_sem.at[slot],
        )

    def add_pair(m):
        for z_lo in range(2):
            pair_copy(m, z_lo, grads[m][2 * z_lo]).wait()
            own_copy(m, z_lo, grads[m][2 * z_lo]).wait()
        stage_copy(m, 0, 0).start()

        @pl.loop(0, 32)
        def _(i):
            slot = lax.rem(i, 2)

            @pl.when(i < 31)
            def _():
                stage_copy(m, i + 1, 1 - slot).start()

            stage_copy(m, i, slot).wait()
            z_lo, t, y_lo, x = split_index(i, (2, 2, 2, 4))
            for z_hi in range(2):
                for r in range(0, 48, 16):
                    place = (z_lo, t, y_lo, x, z_hi, pl.ds(r, 16), slice(None))
                    mine = held[m][place].astype(jnp.float32)
                    other = stage[slot, z_hi, pl.ds(r, 16), pl.ds(0, WIDTHS[m])]
                    held[m][place] = to_low(mine + other.astype(jnp.float32))

    def exchange(m, p, phase, kind):
        axis, whole = RS_ORDERS[p][phase], RS_ORDERS[p][phase + 1 :]
        cols = halves(WIDTHS[m])
        step = 1 if kind % 2 == 0 else -1
        if kind < 2:
            source = moved(me, axis, 2)
            span = cols[kind]
        else:
            source = moved(me, axis, step)
            span = slice(None)
        return pltpu.make_async_remote_copy(
            src_ref=held[m].at[(*cube(source, whole), pl.ds(16 * p, 16), span)],
            dst_ref=boxes[m, p, phase][kind],
            send_sem=send_sem.at[m, p, phase, kind],
            recv_sem=recv_sem.at[m, p, phase, kind],
            device_id=device_at(moved(me, axis, step)),
            device_id_type=MESH,
        )

    def add_boxes(m, p, phase, where, span, kinds):
        whole = RS_ORDERS[p][phase + 1 :]
        dims = lead_of(whole)
        count = 1
        for size in dims:
            count *= size

        @pl.loop(0, count)
        def _(i):
            index = split_index(i, dims)
            place = (*with_index(where, whole, index), pl.ds(16 * p, 16), span)
            total = held[m][place].astype(jnp.float32)
            for kind in kinds:
                total = total + boxes[m, p, phase][kind][index].astype(jnp.float32)
            held[m][place] = to_low(total)

    def run(m, stage_number):
        if stage_number == 0:
            add_pair(m)
            for p in range(3):
                for kind in (0, 1):
                    exchange(m, p, 0, kind).start()
            return
        phase, late = divmod(stage_number - 1, 2)
        for p in range(3):
            axis = RS_ORDERS[p][phase]
            if late == 0:
                for kind, step in ((0, 1), (1, -1)):
                    exchange(m, p, phase, kind).wait_recv()
                    add_boxes(
                        m, p, phase, moved(me, axis, step), halves(WIDTHS[m])[kind], (kind,)
                    )
                    exchange(m, p, phase, 2 + kind).start()
            else:
                for kind in (2, 3):
                    exchange(m, p, phase, kind).wait_recv()
                add_boxes(m, p, phase, me, slice(None), (2, 3))
                if phase < 2:
                    for kind in (0, 1):
                        exchange(m, p, phase + 1, kind).start()
                else:
                    rows = pl.ds(16 * p, 16)
                    sums[m][rows, :] = held[m][(*cube(me, ()), rows, slice(None))]

    for m, stage_number in SEQUENCE:
        run(m, stage_number)
    for m in range(n):
        for p in range(3):
            for phase in range(3):
                for kind in range(4):
                    exchange(m, p, phase, kind).wait_send()


def reduce(grads):
    n = len(WIDTHS)
    dma = pltpu.SemaphoreType.DMA
    flat = [g.reshape(2, 2, 4, 2, 48, w) for group, w in zip(grads, WIDTHS) for g in group]
    outs = pl.pallas_call(
        reduce_kernel,
        out_shape=[jax.ShapeDtypeStruct((48, w), jnp.bfloat16) for w in WIDTHS]
        + [jax.ShapeDtypeStruct((2, 2, 2, 4, 2, 48, w), jnp.bfloat16) for w in WIDTHS],
        in_specs=[pl.BlockSpec(memory_space=pl.ANY)] * (4 * n),
        out_specs=[pl.BlockSpec(memory_space=pltpu.VMEM)] * n
        + [pl.BlockSpec(memory_space=pl.ANY)] * n,
        scratch_shapes=reduce_scratch()
        + [
            pltpu.VMEM((2, 2, 48, WIDE), jnp.bfloat16),
            dma((n, 3, 3, 4)),
            dma((n, 3, 3, 4)),
            dma((n, 2)),
            dma((n, 2)),
            dma((n, 2)),
            dma((2,)),
        ],
        compiler_params=pltpu.CompilerParams(
            collective_id=1, has_side_effects=True, vmem_limit_bytes=63 * 1024 * 1024
        ),
        name="reduce_grads",
    )(*flat)
    return outs[:n]


def normed(values, norm_gain):
    centre = values - jnp.mean(values, axis=-1, keepdims=True)
    spread = jnp.mean(centre * centre, axis=-1, keepdims=True)
    return centre * lax.rsqrt(spread + epsilon) * norm_gain


def gelu_exact(values):
    return jax.nn.gelu(values, approximate=False)


def dot(spec, left, right):
    return jnp.einsum(spec, left, right, preferred_element_type=jnp.float32)


def norm_back(residual, norm_gain, in_grad):
    unused, pullback = jax.vjp(normed, residual, norm_gain)
    return pullback(in_grad)


def attend_forward(residual, gain, weight):
    inputs = to_low(normed(residual, gain))
    projected = to_low(dot("rd,tdc->trc", inputs, weight[:, :, :1152]))
    projected = projected.reshape(2, SEQ, 3, 6, HEAD)
    q, k, v = projected[:, :, 0], projected[:, :, 1], projected[:, :, 2]
    scores = dot("tshd,tuhd->thsu", q, k) * HEAD ** (-0.5)
    peak = jnp.max(scores, axis=-1, keepdims=True)
    log_total = jnp.log(jnp.sum(jnp.exp(scores - peak), axis=-1, keepdims=True)) + peak
    probs = jnp.exp(scores - log_total)
    mixed = to_low(dot("thsu,tuhd->tshd", to_low(probs), v)).reshape(2, SEQ, 384)
    branch = dot("trh,tdh->rd", mixed, weight[:, :, 1152:HALF])
    return residual + branch, (residual, inputs, q, k, v, log_total, mixed)


def attend_backward(stream, gain, weight, saved):
    residual, inputs, q, k, v, log_total, mixed = saved
    scale = HEAD ** (-0.5)
    branch_grad = to_low(stream)
    out_grad = dot("rd,trh->tdh", branch_grad, mixed)
    mixed_grad = to_low(dot("rd,tdh->trh", branch_grad, weight[:, :, 1152:HALF]))
    mixed_grad = mixed_grad.reshape(2, SEQ, 6, HEAD)
    scores = dot("tshd,tuhd->thsu", q, k) * scale
    probs = jnp.exp(scores - log_total)
    v_grad = to_low(dot("thsu,tshd->tuhd", to_low(probs), mixed_grad))
    prob_grad = dot("tshd,tuhd->thsu", mixed_grad, v)
    score_grad = to_low(
        probs * (prob_grad - jnp.sum(probs * prob_grad, axis=-1, keepdims=True))
    )
    q_grad = to_low(dot("thsu,tuhd->tshd", score_grad, k) * scale)
    k_grad = to_low(dot("thsu,tshd->tuhd", score_grad, q) * scale)
    stacked = jnp.stack([q_grad, k_grad, v_grad], axis=2).reshape(2, SEQ, 1152)
    qkv_grad = dot("rd,trc->tdc", inputs, stacked)
    in_grad = dot("trc,tdc->rd", stacked, weight[:, :, :1152])
    residual_grad, gain_grad = norm_back(residual, gain, in_grad)
    return stream + residual_grad, gain_grad, to_low(jnp.concatenate([qkv_grad, out_grad], axis=2))


def dense_forward(residual, gain, up, down):
    inputs = to_low(normed(residual, gain))
    pre = dot("rd,tdf->trf", inputs, up[:, :, :HALF])
    act = to_low(gelu_exact(pre))
    branch = dot("trf,tdf->rd", act, down[:, :, :HALF])
    return residual + branch, (residual, inputs, pre, act)


def dense_backward(stream, gain, up, down, saved):
    residual, inputs, pre, act = saved
    branch_grad = to_low(stream)
    down_grad = dot("rd,trf->tdf", branch_grad, act)
    act_grad = dot("rd,tdf->trf", branch_grad, down[:, :, :HALF])
    unused, pullback = jax.vjp(gelu_exact, pre)
    pre_grad = to_low(pullback(act_grad)[0])
    up_grad = dot("rd,trf->tdf", inputs, pre_grad)
    in_grad = dot("trf,tdf->rd", pre_grad, up[:, :, :HALF])
    residual_grad, gain_grad = norm_back(residual, gain, in_grad)
    return stream + residual_grad, gain_grad, to_low(up_grad), to_low(down_grad)


def experts_both(residual, gain, router, up, down, routes, cotangent):
    inputs = to_low(normed(residual, gain))
    probs = jax.nn.softmax(dot("rd,de->re", inputs, router), axis=-1)
    labels = jnp.arange(4, dtype=jnp.int32)
    chosen = jnp.sum((routes[:, :, None] == labels).astype(jnp.float32), axis=1)
    combine = probs * chosen
    bg = cotangent
    branch = jnp.zeros((SEQ, D), jnp.float32)
    in_grad = jnp.zeros((SEQ, D), jnp.float32)
    combine_grad = []
    up_grads, down_grads = [], []
    for e in range(4):
        pre = dot("rd,tdf->trf", inputs, up[e])
        act = to_low(gelu_exact(pre))
        out = dot("trf,tdf->rd", act, down[e])
        gate = combine[:, e : e + 1]
        branch = branch + gate * out
        combine_grad.append(jnp.sum(out * bg.astype(jnp.float32), axis=-1))
        out_grad = to_low(gate * bg)
        down_grads.append(to_low(dot("rd,trf->tdf", out_grad, act)))
        act_grad = dot("rd,tdf->trf", out_grad, down[e])
        unused, pullback = jax.vjp(gelu_exact, pre)
        pre_grad = to_low(pullback(act_grad)[0])
        up_grads.append(to_low(dot("rd,trf->tdf", inputs, pre_grad)))
        in_grad = in_grad + dot("trf,tdf->rd", pre_grad, up[e])
    probs_grad = jnp.stack(combine_grad, axis=1) * chosen
    logit_grad = probs * (probs_grad - jnp.sum(probs * probs_grad, axis=-1, keepdims=True))
    router_grad = jnp.einsum(
        "rd,re->de", inputs.astype(jnp.float32), logit_grad, precision=precise
    )
    in_grad = in_grad + jnp.einsum(
        "re,de->rd", logit_grad, router.astype(jnp.float32), precision=precise
    )
    residual_grad, gain_grad = norm_back(residual, gain, in_grad)
    stream = cotangent.astype(jnp.float32) + residual_grad
    return to_low(residual + branch), stream, gain_grad, router_grad, up_grads, down_grads


def body(
    activations,
    attn_gain,
    qkv_weight,
    out_weight,
    ffn_gain,
    mlp_up,
    mlp_down,
    router,
    expert_up,
    expert_down,
    routes,
    cotangent,
):
    small = jnp.concatenate([attn_gain.T, ffn_gain.T, router], axis=1)
    small = jnp.pad(small, ((0, 0), (0, SMALL - 8)))
    out_t = jnp.transpose(out_weight, (0, 2, 1))
    attn = [
        jnp.concatenate([qkv_weight[b, 0], qkv_weight[b, 1], qkv_weight[b, 2], out_t[b]], axis=1)
        for b in range(2)
    ]
    sets = jnp.stack([attn[0], mlp_up, mlp_down.T, attn[1]])
    sets = jnp.concatenate(
        [
            sets,
            jnp.broadcast_to(small, (4, *small.shape)),
            expert_up,
            jnp.transpose(expert_down, (0, 2, 1)),
        ],
        axis=2,
    )
    sets = lax.all_to_all(
        sets, "fsdp", split_axis=0, concat_axis=0, tiled=True, axis_index_groups=GROUPS
    )
    sets = sets.reshape(48, WIDE + 2 * HALF)
    shards = [sets[:, :WIDE], sets[:, WIDE : WIDE + HALF], sets[:, WIDE + HALF :]]
    base, ups, downs = [
        whole.reshape(4, 2, D, w) for whole, w in zip(gather(shards), WIDTHS)
    ]
    small = base[0, 0, :, HALF : HALF + 8]
    gains = small[:, :4].astype(jnp.float32).T
    router_full = small[:, 4:8]
    half = lax.axis_index("tp")
    my_routes = lax.dynamic_slice_in_dim(routes, half * SEQ, SEQ, 0)

    residual = activations.astype(jnp.float32)
    residual, saved_first = attend_forward(residual, gains[0], base[0])
    residual, saved_dense = dense_forward(residual, gains[2], base[1], base[2])
    residual, saved_second = attend_forward(residual, gains[1], base[3])
    result, stream, ffn1, router_grad, up_grads, down_grads = experts_both(
        residual, gains[3], router_full, ups, downs, my_routes, cotangent
    )
    stream, attn1, second = attend_backward(stream, gains[1], base[3], saved_second)
    stream, ffn0, up_grad, down_grad = dense_backward(
        stream, gains[2], base[1], base[2], saved_dense
    )
    stream, attn0, first = attend_backward(stream, gains[0], base[0], saved_first)
    tail = jnp.concatenate([jnp.stack([attn0, attn1, ffn0, ffn1], axis=1), router_grad], axis=1)
    tail = to_low(jnp.pad(tail, ((0, 0), (0, SMALL - 8))))
    tail = jnp.broadcast_to(tail, (2, D, SMALL))
    blank = jnp.zeros_like(tail)
    group = [
        jnp.concatenate([first, tail], axis=2),
        jnp.concatenate([up_grad, blank], axis=2),
        jnp.concatenate([down_grad, blank], axis=2),
        jnp.concatenate([second, blank], axis=2),
    ]
    sums = reduce([group, up_grads, down_grads])
    sums = jnp.concatenate(sums, axis=1).reshape(4, 12, WIDE + 2 * HALF)
    sums = lax.all_to_all(
        sums, "fsdp", split_axis=0, concat_axis=0, tiled=True, axis_index_groups=GROUPS
    ).astype(jnp.float32)
    blocks = [sums[0, :, :HALF], sums[3, :, :HALF]]
    qkv_grad = jnp.stack(
        [jnp.stack([b[:, 384 * c : 384 * c + 384] for c in range(3)]) for b in blocks]
    )
    out_grad = jnp.stack([b[:, 1152:].T for b in blocks])
    tail = sums[0, :, HALF:WIDE]
    return (
        result,
        stream,
        tail[:, 0:2].T,
        qkv_grad,
        out_grad,
        tail[:, 2:4].T,
        sums[1, :, :HALF],
        sums[2, :, :HALF].T,
        tail[:, 4:8],
        sums[:, :, WIDE : WIDE + HALF],
        jnp.transpose(sums[:, :, WIDE + HALF :], (0, 2, 1)),
    )


def solution(mesh):
    placed = (
        P(("fsdp", "tp"), None),
        P(None, "fsdp"),
        P(None, None, "fsdp", "tp"),
        P(None, "tp", "fsdp"),
        P(None, "fsdp"),
        P("fsdp", "tp"),
        P("tp", "fsdp"),
        P("fsdp", None),
        P(None, "fsdp", "tp"),
        P(None, "tp", "fsdp"),
        P("fsdp", None),
        P(("fsdp", "tp"), None),
    )
    return jax.shard_map(
        body,
        mesh=mesh,
        in_specs=placed,
        out_specs=(
            P(("fsdp", "tp"), None),
            P(("fsdp", "tp"), None),
            P(None, "fsdp"),
            P(None, None, "fsdp", "tp"),
            P(None, "tp", "fsdp"),
            P(None, "fsdp"),
            P("fsdp", "tp"),
            P("tp", "fsdp"),
            P("fsdp", None),
            P(None, "fsdp", "tp"),
            P(None, "tp", "fsdp"),
        ),
        check_vma=False,
    )
```

```python
import functools
import itertools

import jax
import jax.numpy as jnp
from jax import lax
from jax.experimental import pallas as pl
from jax.experimental.pallas import tpu as pltpu
from jax.sharding import PartitionSpec as P

HEAD = 64
SEQ = 197
D = 768
HALF = 1536
SMALL = 128
WIDE = HALF + SMALL
MESH = pl.DeviceIdType.MESH
GROUPS = [[4 * k + j for j in range(4)] for k in range(16)]

epsilon = 1e-06
precise = lax.Precision.HIGHEST

ORDERS = (("x", "y", "z"), ("y", "z", "x"), ("z", "x", "y"))
WIDTHS = (WIDE, HALF, HALF)


def to_low(values):
    return values.astype(jnp.bfloat16)


def coordinates():
    f, t = lax.axis_index("fsdp"), lax.axis_index("tp")
    return {
        "x": lax.rem(lax.div(f, 8), 4),
        "y": 2 * t + lax.div(f, 32),
        "z": lax.rem(lax.div(f, 2), 4),
        "c": lax.rem(f, 2),
    }


def device_at(place):
    y = place["y"]
    f = ((lax.rem(y, 2) * 4 + place["x"]) * 4 + place["z"]) * 2 + place["c"]
    return (f, lax.div(y, 2))


def moved(place, axis, steps):
    return {**place, axis: lax.rem(place[axis] + steps + 4, 4)}


def greet(place):
    others = [device_at(moved(place, a, s)) for a in "xyz" for s in (1, -1)]
    others.append(device_at({**place, "c": 1 - place["c"]}))
    barrier = pltpu.get_barrier_semaphore()
    for other in others:
        pl.semaphore_signal(barrier, inc=1, device_id=other, device_id_type=MESH)
    pl.semaphore_wait(barrier, len(others))


def cube(where, whole):
    every = slice(None)
    y = (every, every) if "y" in whole else (lax.div(where["y"], 2), lax.rem(where["y"], 2))
    z = (every, every) if "z" in whole else (lax.rem(where["z"], 2), lax.div(where["z"], 2))
    x = every if "x" in whole else where["x"]
    return (z[0], y[0], y[1], x, z[1])


def halves(width):
    first = (width // 256) * 128
    if width - first > first:
        first = width - first
    return (slice(0, first), slice(first, width))


def remote(src, dst, send, recv, target):
    return pltpu.make_async_remote_copy(
        src_ref=src,
        dst_ref=dst,
        send_sem=send,
        recv_sem=recv,
        device_id=device_at(target),
        device_id_type=MESH,
    )


class Gather:
    def __init__(self, me, items, sems):
        self.me, self.items = me, items
        self.send, self.recv, self.send_pair, self.recv_pair, self.own = sems
        self.sibling = {**me, "c": 1 - me["c"]}

    def block(self, i, p, where, whole, cols):
        z_lo, t, y_lo, x, z_hi = cube(where, whole)
        rows = pl.ds(16 * p, 16)
        return self.items[i][1].at[z_lo, self.me["c"], t, y_lo, x, z_hi, rows, cols]

    def mine(self, i):
        z_lo, t, y_lo, x, z_hi = cube(self.me, ())
        return self.items[i][1].at[z_lo, self.me["c"], t, y_lo, x, z_hi, :, self.items[i][2]]

    def own_copy(self, i):
        shard, _, cols = self.items[i]
        return pltpu.make_async_copy(shard.at[:, cols], self.mine(i), self.own.at[i])

    def hop(self, i, p, phase, kind):
        axis, done = ORDERS[p][phase], ORDERS[p][:phase]
        cols = self.items[i][2]
        step = 1 if kind % 2 == 0 else -1
        if kind < 2:
            dst = self.block(i, p, self.me, done, cols)
            src = dst
            if phase == 0:
                src = self.items[i][0].at[pl.ds(16 * p, 16), cols]
        else:
            part = halves(cols.stop - cols.start)[kind - 2]
            span = slice(cols.start + part.start, cols.start + part.stop)
            src = dst = self.block(i, p, moved(self.me, axis, -step), done, span)
        send, recv = self.send.at[i, p, phase, kind], self.recv.at[i, p, phase, kind]
        return remote(src, dst, send, recv, moved(self.me, axis, step))

    def across(self, i, slot):
        send, recv = self.send_pair.at[i, slot], self.recv_pair.at[i, slot]
        shard, _, cols = self.items[i]
        if slot == 0:
            return remote(shard.at[:, cols], self.mine(i), send, recv, self.sibling)
        phase, p, which = (slot - 1) // 9, (slot - 1) // 3 % 3, (slot - 1) % 3
        axis, done = ORDERS[p][phase], ORDERS[p][:phase]
        part = self.block(i, p, moved(self.me, axis, (-1, 1, 2)[which]), done, cols)
        return remote(part, part, send, recv, self.sibling)

    def advance(self, i, stage):
        if stage == 0:
            self.own_copy(i).start()
            self.across(i, 0).start()
        phase, late = divmod(stage, 2)
        if late == 0:
            if phase > 0:
                for p in range(3):
                    for kind in (2, 3):
                        self.hop(i, p, phase - 1, kind).wait_recv()
                    if phase < 3:
                        for kind in (0, 1):
                            if phase == 1 and p == 0 and kind == 0:
                                self.own_copy(i).wait()
                            self.hop(i, p, phase, kind).start()
                    self.across(i, 9 * (phase - 1) + 3 * p + 3).start()
            else:
                for p in range(3):
                    for kind in (0, 1):
                        self.hop(i, p, 0, kind).start()
        else:
            for p in range(3):
                for kind in (0, 1):
                    self.hop(i, p, phase, kind).wait_recv()
                    self.hop(i, p, phase, 2 + kind).start()
                for which in (0, 1):
                    self.across(i, 9 * phase + 3 * p + 1 + which).start()

    def arrived(self, i):
        for slot in range(28):
            self.across(i, slot).wait_recv()

    def drain(self, i):
        for p in range(3):
            for phase in range(3):
                for kind in range(4):
                    self.hop(i, p, phase, kind).wait_send()
        for slot in range(28):
            self.across(i, slot).wait_send()


def gather_sems(n):
    dma = pltpu.SemaphoreType.DMA
    return [dma((n, 3, 3, 4)), dma((n, 3, 3, 4)), dma((n, 28)), dma((n, 28)), dma((n,))]


def gather_kernel(shard, whole, *sems):
    me = coordinates()
    greet(me)
    work = Gather(me, [(shard, whole, slice(0, WIDE))], sems)
    for stage in range(7):
        work.advance(0, stage)
    work.arrived(0)
    work.drain(0)


def gather(shard):
    return pl.pallas_call(
        gather_kernel,
        out_shape=jax.ShapeDtypeStruct((2, 2, 2, 2, 4, 2, 48, WIDE), jnp.bfloat16),
        in_specs=[pl.BlockSpec(memory_space=pl.ANY)],
        out_specs=pl.BlockSpec(memory_space=pl.ANY),
        scratch_shapes=gather_sems(1),
        compiler_params=pltpu.CompilerParams(collective_id=0, has_side_effects=True),
        name="gather_weights",
    )(shard)

def lead_of(whole):
    dims = []
    if "z" in whole:
        dims.append(2)
    if "y" in whole:
        dims += [2, 2]
    if "x" in whole:
        dims.append(4)
    if "z" in whole:
        dims.append(2)
    return tuple(dims)


def split_index(i, dims):
    out = []
    for size in reversed(dims):
        out.append(lax.rem(i, size))
        i = lax.div(i, size)
    return tuple(reversed(out))


def with_index(where, whole, index):
    rest = list(index)
    full = list(cube(where, whole))
    for place, value in enumerate(full):
        if isinstance(value, slice):
            full[place] = rest.pop(0)
    return tuple(full)


RS_ORDERS = tuple(tuple(reversed(order)) for order in ORDERS)


class Reduce:
    def __init__(self, me, widths, grads, landing, held, boxes, sums, stage, sems):
        self.me, self.widths, self.grads, self.landing = me, widths, grads, landing
        self.held, self.boxes, self.sums, self.stage = held, boxes, sums, stage
        self.send, self.recv, self.send_pair, self.recv_pair, self.own, self.stage_sem = sems
        self.sibling = {**me, "c": 1 - me["c"]}

    def own_copy(self, m, z_lo):
        src = self.grads[m].at[z_lo, self.me["c"]]
        return pltpu.make_async_copy(src, self.held[m].at[z_lo], self.own.at[m, z_lo])

    def pair_copy(self, m, z_lo):
        return remote(
            self.grads[m].at[z_lo, 1 - self.me["c"]],
            self.landing[m].at[z_lo],
            self.send_pair.at[m, z_lo],
            self.recv_pair.at[m, z_lo],
            self.sibling,
        )

    def begin(self, m):
        for z_lo in range(2):
            self.pair_copy(m, z_lo).start()
            self.own_copy(m, z_lo).start()

    def stage_copy(self, m, i, slot):
        z_lo, t, y_lo, x = split_index(i, (2, 2, 2, 4))
        return pltpu.make_async_copy(
            self.landing[m].at[z_lo, t, y_lo, x],
            self.stage.at[slot, :, :, pl.ds(0, self.widths[m])],
            self.stage_sem.at[slot],
        )

    def add_pair(self, m):
        held, stage = self.held[m], self.stage
        for z_lo in range(2):
            self.pair_copy(m, z_lo).wait()
            self.own_copy(m, z_lo).wait()
        self.stage_copy(m, 0, 0).start()

        @pl.loop(0, 32)
        def _(i):
            slot = lax.rem(i, 2)

            @pl.when(i < 31)
            def _():
                self.stage_copy(m, i + 1, 1 - slot).start()

            self.stage_copy(m, i, slot).wait()
            z_lo, t, y_lo, x = split_index(i, (2, 2, 2, 4))
            for z_hi in range(2):
                for r in range(0, 48, 16):
                    place = (z_lo, t, y_lo, x, z_hi, pl.ds(r, 16), slice(None))
                    mine = held[place].astype(jnp.float32)
                    other = stage[slot, z_hi, pl.ds(r, 16), pl.ds(0, self.widths[m])]
                    held[place] = to_low(mine + other.astype(jnp.float32))

    def exchange(self, m, p, phase, kind):
        axis, whole = RS_ORDERS[p][phase], RS_ORDERS[p][phase + 1 :]
        step = 1 if kind % 2 == 0 else -1
        if kind < 2:
            source = moved(self.me, axis, 2)
            span = halves(self.widths[m])[kind]
        else:
            source = moved(self.me, axis, step)
            span = slice(None)
        return remote(
            self.held[m].at[(*cube(source, whole), pl.ds(16 * p, 16), span)],
            self.boxes[m, p, phase][kind],
            self.send.at[m, p, phase, kind],
            self.recv.at[m, p, phase, kind],
            moved(self.me, axis, step),
        )

    def add_boxes(self, m, p, phase, where, span, kinds):
        whole = RS_ORDERS[p][phase + 1 :]
        dims = lead_of(whole)
        count = 1
        for size in dims:
            count *= size
        held = self.held[m]

        @pl.loop(0, count)
        def _(i):
            index = split_index(i, dims)
            place = (*with_index(where, whole, index), pl.ds(16 * p, 16), span)
            total = held[place].astype(jnp.float32)
            for kind in kinds:
                total = total + self.boxes[m, p, phase][kind][index].astype(jnp.float32)
            held[place] = to_low(total)

    def run(self, m, stage_number):
        if stage_number == 0:
            self.add_pair(m)
            for p in range(3):
                for kind in (0, 1):
                    self.exchange(m, p, 0, kind).start()
            return
        me = self.me
        phase, late = divmod(stage_number - 1, 2)
        for p in range(3):
            axis = RS_ORDERS[p][phase]
            if late == 0:
                for kind, step in ((0, 1), (1, -1)):
                    self.exchange(m, p, phase, kind).wait_recv()
                    span = halves(self.widths[m])[kind]
                    self.add_boxes(m, p, phase, moved(me, axis, step), span, (kind,))
                    self.exchange(m, p, phase, 2 + kind).start()
            else:
                for kind in (2, 3):
                    self.exchange(m, p, phase, kind).wait_recv()
                self.add_boxes(m, p, phase, me, slice(None), (2, 3))
                if phase < 2:
                    for kind in (0, 1):
                        self.exchange(m, p, phase + 1, kind).start()
                else:
                    rows = pl.ds(16 * p, 16)
                    self.sums[m][rows, :] = self.held[m][(*cube(me, ()), rows, slice(None))]

    def drain(self):
        for m in range(len(self.widths)):
            for p in range(3):
                for phase in range(3):
                    for kind in range(4):
                        self.exchange(m, p, phase, kind).wait_send()


def reduce_scratch(widths):
    shapes = []
    for w in widths:
        shapes.append(pltpu.VMEM((2, 2, 2, 4, 2, 48, w), jnp.bfloat16))
        cols = halves(w)
        for p in range(3):
            for phase in range(3):
                lead = lead_of(RS_ORDERS[p][phase + 1 :])
                for part in cols:
                    shapes.append(pltpu.VMEM((*lead, 16, part.stop - part.start), jnp.bfloat16))
                for _ in range(2):
                    shapes.append(pltpu.VMEM((*lead, 16, w), jnp.bfloat16))
    n = len(widths)
    dma = pltpu.SemaphoreType.DMA
    shapes += [
        pltpu.VMEM((2, 2, 48, max(widths)), jnp.bfloat16),
        dma((n, 3, 3, 4)),
        dma((n, 3, 3, 4)),
        dma((n, 2)),
        dma((n, 2)),
        dma((n, 2)),
        dma((2,)),
    ]
    return shapes


def make_reduce(me, widths, grads, landing, sums, refs):
    refs = list(refs)
    held, boxes = [], {}
    for m in range(len(widths)):
        held.append(refs.pop(0))
        for p in range(3):
            for phase in range(3):
                boxes[m, p, phase] = [refs.pop(0) for _ in range(4)]
    return Reduce(me, widths, grads, landing, held, boxes, sums, refs[0], refs[1:])


def landing_shape(w):
    return jax.ShapeDtypeStruct((2, 2, 2, 4, 2, 48, w), jnp.bfloat16)


def reduce_kernel(grad, total, landing, *refs):
    me = coordinates()
    greet(me)
    work = make_reduce(me, (WIDE,), [grad], [landing], [total], refs)
    work.begin(0)
    for stage in range(7):
        work.run(0, stage)
    work.drain()


def reduce(grad):
    return pl.pallas_call(
        reduce_kernel,
        out_shape=[jax.ShapeDtypeStruct((48, WIDE), jnp.bfloat16), landing_shape(WIDE)],
        in_specs=[pl.BlockSpec(memory_space=pl.ANY)],
        out_specs=[pl.BlockSpec(memory_space=pltpu.VMEM), pl.BlockSpec(memory_space=pl.ANY)],
        scratch_shapes=reduce_scratch((WIDE,)),
        compiler_params=pltpu.CompilerParams(
            collective_id=3, has_side_effects=True, vmem_limit_bytes=60 * 1024 * 1024
        ),
        name="reduce_grads",
    )(grad.reshape(2, 2, 2, 2, 4, 2, 48, WIDE))[0]


PAD = 208
SCALE = HEAD ** (-0.5)
FWD_LOADS = ((0, 0), (0, 1), (1, 0), (2, 0), (1, 1), (2, 1), (3, 0), (3, 1))
BWD_LOADS = ((3, 0), (3, 1), (1, 0), (2, 0), (1, 1), (2, 1), (0, 0), (0, 1))


def nn(a, b):
    return lax.dot_general(a, b, (((1,), (0,)), ((), ())), preferred_element_type=jnp.float32)


def nt(a, b):
    return lax.dot_general(a, b, (((1,), (1,)), ((), ())), preferred_element_type=jnp.float32)


def turned(values):
    return to_low(jnp.transpose(values.astype(jnp.float32)))


def norm_parts(s):
    centre = s - jnp.mean(s, axis=-1, keepdims=True)
    r = lax.rsqrt(jnp.mean(centre * centre, axis=-1, keepdims=True) + epsilon)
    return centre * r, r


def norm_low(s, gain):
    return to_low(norm_parts(s)[0] * gain)


def norm_pull(s, gain, in_grad):
    xhat, r = norm_parts(s)
    u = in_grad * gain
    first = jnp.mean(u, axis=-1, keepdims=True)
    second = jnp.mean(u * xhat, axis=-1, keepdims=True)
    return r * (u - first - xhat * second), jnp.sum(xhat * in_grad, axis=0, keepdims=True)


def normal_cdf(x):
    return 0.5 * (1.0 + lax.erf(x * 0.7071067811865476))


def gelu_slope(x, cdf):
    return cdf + x * (0.3989422804014327 * jnp.exp(-0.5 * x * x))


def head_masks():
    lane = lax.broadcasted_iota(jnp.int32, (PAD, 128), 1)
    return lane < HEAD, lane >= HEAD


def probabilities(q, k):
    scores = nt(q, k) * SCALE
    key = lax.broadcasted_iota(jnp.int32, scores.shape, 1)
    scores = jnp.where(key < SEQ, scores, -1e30)
    scores = jnp.exp(scores - jnp.max(scores, axis=-1, keepdims=True))
    return scores / jnp.sum(scores, axis=-1, keepdims=True)


def lanes(start):
    return pl.ds(pl.multiple_of(start, 128), 128)


def attend_forward(res, gain, weight, x_s, qkv, mixed, out):
    x_s[...] = norm_low(res[...], gain)
    x = x_s[...]
    for t in range(2):
        qkv[t, :, :] = to_low(nn(x, weight[t][:, :1152]))
        yield
    for t in range(2):

        @pl.loop(0, 3)
        def _(pair):
            at = pair * 128
            q, k, v = [qkv[t, :, lanes(at + 384 * j)] for j in range(3)]
            parts = []
            for mask in head_masks():
                probs = probabilities(jnp.where(mask, q, jnp.zeros_like(q)), k)
                parts.append(nn(to_low(probs), v))
            mixed[t, :, lanes(at)] = to_low(jnp.where(head_masks()[0], parts[0], parts[1]))

        yield
    total = res[...]
    for t in range(2):
        total = total + nt(mixed[t], weight[t][:, 1152:HALF])
    out[...] = total
    yield


def dense_forward(res, gain, up, down, x_s, out, t):
    if t == 0:
        x_s[...] = norm_low(res[...], gain)
        out[...] = res[...]
    for j in range(0, HALF, 512):
        pre = nn(x_s[...], up[:, j : j + 512])
        act = to_low(pre * normal_cdf(pre))
        out[...] += nt(act, down[:, j : j + 512])
        yield


def hidden_tile(x, x_t, g, g_t, up, down, put_up, put_down):
    pre = nn(x, up)
    cdf = normal_cdf(pre)
    act = to_low(pre * cdf)
    pre_grad = to_low(gelu_slope(pre, cdf) * nn(g, down))
    put_down(to_low(nn(g_t, act)))
    put_up(to_low(nn(x_t, pre_grad)))
    return nt(act, down), nt(pre_grad, up)


def experts_kernel(*refs):
    (act_in, cot_in, chosen, base, shard_up, shard_down) = refs[:6]
    (whole_up, whole_down, grad_up, grad_down, result, stream, r1, r2) = refs[6:14]
    (qkv0, qkv1, mixed0, mixed1, gain_out, router_out) = refs[14:20]
    (w, res, x_s, x_t, bg, og, og_t, branch, din, cgrad, e_w, e_g, w_sem, small_s, small_sem) = refs[20:35]
    e_sem, g_sem = refs[35:37]
    me = coordinates()
    greet(me)
    items = [
        (shard, whole, slice(at, at + 768))
        for at in (0, 768)
        for shard, whole in ((shard_up, whole_up), (shard_down, whole_down))
    ]
    work = Gather(me, items, refs[37:])

    def load(n):
        s, t = FWD_LOADS[n]
        return pltpu.make_async_copy(base.at[s, t], w.at[n % 4], w_sem.at[n])

    for n in range(4):
        load(n).start()
    for i in range(4):
        work.advance(i, 0)
    small_copy = pltpu.make_async_copy(
        base.at[0, 0, :, pl.ds(HALF, SMALL)], small_s, small_sem.at[0]
    )
    small_copy.start()
    bg[...] = jnp.zeros((PAD, D), jnp.bfloat16)
    bg[0:SEQ, :] = cot_in[...]
    res[...] = jnp.zeros((PAD, D), jnp.float32)
    res[0:SEQ, :] = act_in[...].astype(jnp.float32)
    small_copy.wait()
    rows = jnp.transpose(small_s[...].astype(jnp.float32))
    gains = [rows[j : j + 1, :] for j in range(4)]

    events = {
        1: ((0, 1), (1, 1), (2, 1), (3, 1)),
        2: ((0, 2), (1, 2), (2, 2), (3, 2)),
        4: ((0, 3), (1, 3), (2, 3), (3, 3)),
        5: ((0, 4), (1, 4)),
        14: ((0, 5), (1, 5), (2, 4), (3, 4)),
    }

    def forward():
        load(0).wait()
        load(1).wait()
        yield from attend_forward(res, gains[0], [w.at[0], w.at[1]], x_s, qkv0, mixed0, r1)
        load(4).start()
        load(5).start()
        for t in range(2):
            load(2 + 2 * t).wait()
            load(3 + 2 * t).wait()
            up, down = (w.at[2], w.at[3]) if t == 0 else (w.at[0], w.at[1])
            yield from dense_forward(r1, gains[2], up, down, x_s, r2, t)
            if t == 0:
                load(6).start()
                load(7).start()
        load(6).wait()
        load(7).wait()
        yield from attend_forward(r2, gains[1], [w.at[2], w.at[3]], x_s, qkv1, mixed1, res)

    for n, _ in enumerate(forward()):
        for event in events.get(n + 1, ()):
            work.advance(*event)

    x_s[...] = norm_low(res[...], gains[3])
    x_t[...] = turned(x_s[...])
    lane = lax.broadcasted_iota(jnp.int32, (PAD, 128), 1)
    logits = nn(x_s[...], small_s[...])
    logits = jnp.where((lane >= 4) & (lane < 8), logits, -1e30)
    probs = jnp.exp(logits - jnp.max(logits, axis=-1, keepdims=True))
    probs = probs / jnp.sum(probs, axis=-1, keepdims=True)
    combine = probs * chosen[...]
    branch[...] = res[...]
    din[...] = jnp.zeros((PAD, D), jnp.float32)
    cgrad[...] = jnp.zeros((PAD, 128), jnp.float32)
    for e in range(4):
        gated = combine[:, 4 + e : 5 + e] * bg[...].astype(jnp.float32)
        og[e] = to_low(gated)
        og_t[e] = turned(to_low(gated))

    wholes, grads = (whole_up, whole_down), (grad_up, grad_down)

    def place(i):
        h, e, t = split_index(i, (2, 4, 2))
        return h, e, t, lax.div(e, 2), lax.rem(e, 2)

    def fetch(i, mat):
        h, e, t, z_lo, c = place(i)
        slot = lax.rem(i, 2)
        cols = pl.ds(pl.multiple_of(h * 768, 128), 768)
        return pltpu.make_async_copy(
            wholes[mat].at[z_lo, c, t, :, :, :, :, cols], e_w.at[slot, mat], e_sem.at[slot, mat]
        )

    def store(i, mat):
        h, e, t, _, _ = place(i)
        slot = lax.rem(i, 2)
        cols = pl.ds(pl.multiple_of(h * 768, 128), 768)
        return pltpu.make_async_copy(
            e_g.at[slot, mat], grads[mat].at[e, t, :, cols], g_sem.at[slot, mat]
        )

    @pl.loop(0, 16)
    def _(i):
        slot = lax.rem(i, 2)

        @pl.when(i == 0)
        def _():
            for item in (0, 1):
                work.advance(item, 6)
                work.arrived(item)
            fetch(0, 0).start()
            fetch(0, 1).start()

        @pl.when(i == 6)
        def _():
            for item in (2, 3):
                work.advance(item, 5)

        @pl.when(i == 8)
        def _():
            for item in (2, 3):
                work.advance(item, 6)
                work.arrived(item)
            fetch(8, 0).start()
            fetch(8, 1).start()

        @pl.when((i != 7) & (i != 15))
        def _():
            fetch(i + 1, 0).start()
            fetch(i + 1, 1).start()

        fetch(i, 0).wait()
        fetch(i, 1).wait()

        @pl.when(i >= 2)
        def _():
            store(i - 2, 0).wait()
            store(i - 2, 1).wait()

        h, e, t, _, _ = place(i)
        out = jnp.zeros((PAD, D), jnp.float32)
        back = jnp.zeros((PAD, D), jnp.float32)
        for j in range(0, 768, 256):

            def put(mat, value, j=j):
                e_g[slot, mat, :, j : j + 256] = value

            up = e_w[slot, 0, :, :, :, :, j : j + 256].reshape(D, 256)
            down = e_w[slot, 1, :, :, :, :, j : j + 256].reshape(D, 256)
            a, b = hidden_tile(
                x_s[...], x_t[...], og[e], og_t[e], up, down,
                functools.partial(put, 0), functools.partial(put, 1),
            )
            out, back = out + a, back + b
        store(i, 0).start()
        store(i, 1).start()
        mine = lane == 4 + e
        gate = jnp.sum(jnp.where(mine, combine, 0.0), axis=-1, keepdims=True)
        branch[...] += gate * out
        din[...] += back
        share = jnp.sum(out * bg[...].astype(jnp.float32), axis=-1, keepdims=True)
        cgrad[...] += jnp.where(mine, share, 0.0)

    result[...] = to_low(branch[0:SEQ, :])
    probs_grad = cgrad[...] * chosen[...]
    logit_grad = probs * (probs_grad - jnp.sum(probs * probs_grad, axis=-1, keepdims=True))
    high = to_low(logit_grad)
    rest = to_low(logit_grad - high.astype(jnp.float32))
    router_out[...] = nn(x_t[...], high) + nn(x_t[...], rest)
    in_grad = din[...] + nt(high, small_s[...]) + nt(rest, small_s[...])
    back, gain_grad = norm_pull(res[...], gains[3], in_grad)
    gain_out[...] = gain_grad
    stream[...] = bg[...].astype(jnp.float32) + back
    for i in (14, 15):
        store(i, 0).wait()
        store(i, 1).wait()
    for i in range(4):
        work.drain(i)


def run_experts(activations, cotangent, chosen, base, shard_up, shard_down):
    f32, bf16 = jnp.float32, jnp.bfloat16
    shape = jax.ShapeDtypeStruct
    vmem, hbm = pl.BlockSpec(memory_space=pltpu.VMEM), pl.BlockSpec(memory_space=pl.ANY)
    dma = pltpu.SemaphoreType.DMA
    cubes = shape((2, 2, 2, 2, 4, 2, 48, HALF), bf16)
    return pl.pallas_call(
        experts_kernel,
        out_shape=[
            cubes,
            cubes,
            shape((4, 2, D, HALF), bf16),
            shape((4, 2, D, HALF), bf16),
            shape((SEQ, D), bf16),
            shape((PAD, D), f32),
            shape((PAD, D), f32),
            shape((PAD, D), f32),
            shape((2, PAD, 1152), bf16),
            shape((2, PAD, 1152), bf16),
            shape((2, PAD, 384), bf16),
            shape((2, PAD, 384), bf16),
            shape((1, D), f32),
            shape((D, 128), f32),
        ],
        in_specs=[vmem, vmem, vmem, hbm, hbm, hbm],
        out_specs=[hbm] * 4 + [vmem] * 10,
        scratch_shapes=[
            pltpu.VMEM((4, D, WIDE), bf16),
            pltpu.VMEM((PAD, D), f32),
            pltpu.VMEM((PAD, D), bf16),
            pltpu.VMEM((D, PAD), bf16),
            pltpu.VMEM((PAD, D), bf16),
            pltpu.VMEM((4, PAD, D), bf16),
            pltpu.VMEM((4, D, PAD), bf16),
            pltpu.VMEM((PAD, D), f32),
            pltpu.VMEM((PAD, D), f32),
            pltpu.VMEM((PAD, 128), f32),
            pltpu.VMEM((2, 2, 2, 4, 2, 48, 768), bf16),
            pltpu.VMEM((2, 2, D, 768), bf16),
            dma((8,)),
            pltpu.VMEM((D, 128), bf16),
            dma((1,)),
            dma((2, 2)),
            dma((2, 2)),
            *gather_sems(4),
        ],
        compiler_params=pltpu.CompilerParams(
            collective_id=1, has_side_effects=True, vmem_limit_bytes=60 * 1024 * 1024
        ),
        name="forward_experts",
    )(activations, cotangent, chosen, base, shard_up, shard_down)


def attend_backward(stream, res, gain, weight, qkv, mixed, s, tools, put_gain):
    x_s, x_t, bg, bg_t, din, dmix, dqkv, grad_slot, grad_send = tools
    bg[...] = to_low(stream[...])
    bg_t[...] = turned(bg[...])
    x_s[...] = norm_low(res[...].astype(jnp.float32), gain)
    x_t[...] = turned(x_s[...])
    yield
    for t in range(2):
        dmix[...] = to_low(nn(bg[...], weight[t][:, 1152:HALF]))

        @pl.loop(0, 3)
        def _(pair):
            at = pair * 128
            q, k, v = [qkv[t, :, lanes(at + 384 * j)] for j in range(3)]
            m = dmix[:, lanes(at)]
            parts = []
            for mask in head_masks():
                probs = probabilities(jnp.where(mask, q, jnp.zeros_like(q)), k)
                prob_grad = nt(jnp.where(mask, m, jnp.zeros_like(m)), v)
                inner = jnp.sum(probs * prob_grad, axis=-1, keepdims=True)
                score_grad = probs * (prob_grad - inner)
                v_grad = nn(turned(to_low(probs)), m)
                q_grad = nn(to_low(score_grad), k) * SCALE
                k_grad = nn(turned(to_low(score_grad)), q) * SCALE
                parts.append((q_grad, k_grad, v_grad))
            for j in range(3):
                both = jnp.where(head_masks()[0], parts[0][j], parts[1][j])
                dqkv[:, lanes(at + 384 * j)] = to_low(both)

        yield
        slot = grad_slot(s, t)
        slot[:, 1152:HALF] = to_low(nn(bg_t[...], mixed[t]))
        for j in range(0, 1152, 384):
            slot[:, j : j + 384] = to_low(nn(x_t[...], dqkv[:, j : j + 384]))
        grad_send(s, t)
        part = nt(dqkv[...], weight[t][:, :1152])
        if t == 0:
            din[...] = part
        else:
            din[...] += part
        yield
    back, gain_grad = norm_pull(res[...].astype(jnp.float32), gain, din[...])
    stream[...] += back
    put_gain(gain_grad)
    yield


def dense_backward(stream, res, gain, up, down, t, tools, put_gain):
    x_s, x_t, bg, bg_t, din, dmix, dqkv, grad_slot, grad_send = tools
    if t == 0:
        bg[...] = to_low(stream[...])
        bg_t[...] = turned(bg[...])
        x_s[...] = norm_low(res[...], gain)
        x_t[...] = turned(x_s[...])
        din[...] = jnp.zeros((PAD, D), jnp.float32)
        yield
    slots = grad_slot(1, t), grad_slot(2, t)

    @pl.loop(0, 3)
    def _(n):
        back = jnp.zeros((PAD, D), jnp.float32)
        for half in range(2):
            cols = pl.ds(pl.multiple_of(n * 512 + 256 * half, 128), 256)
            pre = nn(x_s[...], up[:, cols])
            cdf = normal_cdf(pre)
            act = to_low(pre * cdf)
            pre_grad = to_low(gelu_slope(pre, cdf) * nn(bg[...], down[:, cols]))
            slots[0][:, cols] = to_low(nn(x_t[...], pre_grad))
            slots[1][:, cols] = to_low(nn(bg_t[...], act))
            back = back + nt(pre_grad, up[:, cols])
        din[...] += back

    grad_send(1, t)
    grad_send(2, t)
    yield
    if t == 1:
        back, gain_grad = norm_pull(res[...], gain, din[...])
        stream[...] += back
        put_gain(gain_grad)
        yield


BWD_EVENTS = {
    4: ((0, 0),),
    6: ((0, 1), (1, 0)),
    8: ((0, 2),),
    9: ((1, 1),),
    10: ((0, 3),),
    11: ((0, 4), (0, 5)),
    12: ((1, 2), (0, 6)),
    13: ((1, 3),),
    14: ((1, 4),),
    15: ((1, 5),),
}


def backward_kernel(*refs):
    (act_in, base, stream_in, r1, r2) = refs[:5]
    (qkv0, qkv1, mixed0, mixed1, gain_in, router_in, grad_up, grad_down) = refs[5:13]
    (grads, stream_out, sum_up, sum_down, land_up, land_down) = refs[13:19]
    (w, g, stream, res0, x_s, x_t, bg, bg_t, din, dmix, dqkv, rows_s, small_s) = refs[19:32]
    w_sem, g_sem, small_sem = refs[32:35]
    me = coordinates()
    greet(me)
    work = make_reduce(
        me,
        (HALF, HALF),
        [grad_up, grad_down],
        [land_up, land_down],
        [sum_up, sum_down],
        refs[35:],
    )

    def load(n):
        s, t = BWD_LOADS[n]
        return pltpu.make_async_copy(base.at[s, t], w.at[n % 3], w_sem.at[n])

    for n in range(3):
        load(n).start()
    work.begin(0)
    work.begin(1)
    small_copy = pltpu.make_async_copy(
        base.at[0, 0, :, pl.ds(HALF, SMALL)], small_s, small_sem.at[0]
    )
    small_copy.start()
    stream[...] = stream_in[...]
    res0[...] = jnp.zeros((PAD, D), jnp.bfloat16)
    res0[0:SEQ, :] = act_in[...]
    small_copy.wait()
    turned_small = jnp.transpose(small_s[...].astype(jnp.float32))
    gains = [turned_small[j : j + 1, :] for j in range(4)]
    rows_s[...] = jnp.zeros((128, D), jnp.float32)
    rows_s[3:4, :] = gain_in[...]

    order = [(3, 0), (3, 1), (1, 0), (2, 0), (1, 1), (2, 1), (0, 0), (0, 1)]

    def send_copy(s, t):
        n = order.index((s, t))
        return pltpu.make_async_copy(g.at[n % 2], grads.at[s, t], g_sem.at[n])

    def grad_slot(s, t):
        n = order.index((s, t))
        if n >= 2:
            send_copy(*order[n - 2]).wait()
        return g.at[n % 2]

    def grad_send(s, t):
        if (s, t) in ((0, 0), (0, 1)):
            return
        send_copy(s, t).start()

    tools = (x_s, x_t, bg, bg_t, din, dmix, dqkv, grad_slot, grad_send)

    def put_gain(j, value):
        rows_s[j : j + 1, :] = value

    g[...] = jnp.zeros(g.shape, jnp.bfloat16)

    def backward():
        load(0).wait()
        load(1).wait()
        yield from attend_backward(
            stream, r2, gains[1], [w.at[0], w.at[1]], qkv1, mixed1, 3, tools,
            functools.partial(put_gain, 1),
        )
        load(3).start()
        load(4).start()
        load(2).wait()
        load(3).wait()
        put = functools.partial(put_gain, 2)
        yield from dense_backward(stream, r1, gains[2], w.at[2], w.at[0], 0, tools, put)
        load(5).start()
        load(6).start()
        load(4).wait()
        load(5).wait()
        yield from dense_backward(stream, r1, gains[2], w.at[1], w.at[2], 1, tools, put)
        load(7).start()
        load(6).wait()
        load(7).wait()
        yield from attend_backward(
            stream, res0, gains[0], [w.at[0], w.at[1]], qkv0, mixed0, 0, tools,
            functools.partial(put_gain, 0),
        )

    for n, _ in enumerate(backward()):
        for event in BWD_EVENTS.get(n + 1, ()):
            work.run(*event)
    tail = to_low(jnp.transpose(rows_s[...]) + router_in[...])
    for t in range(2):
        g[t, :, HALF:WIDE] = tail
        send_copy(0, t).start()
    stream_out[...] = stream[0:SEQ, :]
    work.run(1, 6)
    for t in range(2):
        send_copy(0, t).wait()
    work.drain()


def run_backward(*args):
    f32, bf16 = jnp.float32, jnp.bfloat16
    shape = jax.ShapeDtypeStruct
    vmem, hbm = pl.BlockSpec(memory_space=pltpu.VMEM), pl.BlockSpec(memory_space=pl.ANY)
    dma = pltpu.SemaphoreType.DMA
    cubes = [a.reshape(2, 2, 2, 2, 4, 2, 48, HALF) for a in args[-2:]]
    return pl.pallas_call(
        backward_kernel,
        out_shape=[
            shape((4, 2, D, WIDE), bf16),
            shape((SEQ, D), f32),
            shape((48, HALF), bf16),
            shape((48, HALF), bf16),
            landing_shape(HALF),
            landing_shape(HALF),
        ],
        in_specs=[vmem, hbm] + [vmem] * 9 + [hbm] * 2,
        out_specs=[hbm, vmem, vmem, vmem, hbm, hbm],
        scratch_shapes=[
            pltpu.VMEM((3, D, WIDE), bf16),
            pltpu.VMEM((2, D, WIDE), bf16),
            pltpu.VMEM((PAD, D), f32),
            pltpu.VMEM((PAD, D), bf16),
            pltpu.VMEM((PAD, D), bf16),
            pltpu.VMEM((D, PAD), bf16),
            pltpu.VMEM((PAD, D), bf16),
            pltpu.VMEM((D, PAD), bf16),
            pltpu.VMEM((PAD, D), f32),
            pltpu.VMEM((PAD, 384), bf16),
            pltpu.VMEM((PAD, 1152), bf16),
            pltpu.VMEM((128, D), f32),
            pltpu.VMEM((D, 128), bf16),
            dma((8,)),
            dma((8,)),
            dma((1,)),
            *reduce_scratch((HALF, HALF)),
        ],
        compiler_params=pltpu.CompilerParams(
            collective_id=2, has_side_effects=True, vmem_limit_bytes=63 * 1024 * 1024
        ),
        name="backward_reduce",
    )(*args[:-2], *cubes)


def body(
    activations,
    attn_gain,
    qkv_weight,
    out_weight,
    ffn_gain,
    mlp_up,
    mlp_down,
    router,
    expert_up,
    expert_down,
    routes,
    cotangent,
):
    small = jnp.concatenate([attn_gain.T, ffn_gain.T, router], axis=1)
    small = jnp.pad(small, ((0, 0), (0, SMALL - 8)))
    out_t = jnp.transpose(out_weight, (0, 2, 1))
    attn = [
        jnp.concatenate([qkv_weight[b, 0], qkv_weight[b, 1], qkv_weight[b, 2], out_t[b]], axis=1)
        for b in range(2)
    ]
    sets = jnp.stack([attn[0], mlp_up, mlp_down.T, attn[1]])
    sets = jnp.concatenate(
        [
            sets,
            jnp.broadcast_to(small, (4, *small.shape)),
            expert_up,
            jnp.transpose(expert_down, (0, 2, 1)),
        ],
        axis=2,
    )
    sets = lax.all_to_all(
        sets, "fsdp", split_axis=0, concat_axis=0, tiled=True, axis_index_groups=GROUPS
    )
    sets = sets.reshape(48, WIDE + 2 * HALF)
    shards = [sets[:, :WIDE], sets[:, WIDE : WIDE + HALF], sets[:, WIDE + HALF :]]
    base = gather(shards[0]).reshape(4, 2, D, WIDE)
    half = lax.axis_index("tp")
    my_routes = lax.dynamic_slice_in_dim(routes, half * SEQ, SEQ, 0)
    labels = jnp.arange(-4, 124, dtype=jnp.int32)
    chosen = jnp.sum((my_routes[:, :, None] == labels).astype(jnp.float32), axis=1)
    chosen = jnp.pad(chosen, ((0, PAD - SEQ), (0, 0)))
    outs = run_experts(activations, cotangent, chosen, base, shards[1], shards[2])
    grad_up, grad_down, result, stream, r1, r2 = outs[2:8]
    qkv0, qkv1, mixed0, mixed1, gain_grad, router_grad = outs[8:]
    grads, stream, sum_up, sum_down, _, _ = run_backward(
        activations, base, stream, r1, r2, qkv0, qkv1, mixed0, mixed1, gain_grad, router_grad,
        grad_up, grad_down,
    )
    sums = jnp.concatenate([reduce(grads), sum_up, sum_down], axis=1)
    sums = sums.reshape(4, 12, WIDE + 2 * HALF)
    sums = lax.all_to_all(
        sums, "fsdp", split_axis=0, concat_axis=0, tiled=True, axis_index_groups=GROUPS
    ).astype(jnp.float32)
    blocks = [sums[0, :, :HALF], sums[3, :, :HALF]]
    qkv_grad = jnp.stack(
        [jnp.stack([b[:, 384 * c : 384 * c + 384] for c in range(3)]) for b in blocks]
    )
    out_grad = jnp.stack([b[:, 1152:].T for b in blocks])
    tail = sums[0, :, HALF:WIDE]
    return (
        result,
        stream,
        tail[:, 0:2].T,
        qkv_grad,
        out_grad,
        tail[:, 2:4].T,
        sums[1, :, :HALF],
        sums[2, :, :HALF].T,
        tail[:, 4:8],
        sums[:, :, WIDE : WIDE + HALF],
        jnp.transpose(sums[:, :, WIDE + HALF :], (0, 2, 1)),
    )


def solution(mesh):
    placed = (
        P(("fsdp", "tp"), None),
        P(None, "fsdp"),
        P(None, None, "fsdp", "tp"),
        P(None, "tp", "fsdp"),
        P(None, "fsdp"),
        P("fsdp", "tp"),
        P("tp", "fsdp"),
        P("fsdp", None),
        P(None, "fsdp", "tp"),
        P(None, "tp", "fsdp"),
        P("fsdp", None),
        P(("fsdp", "tp"), None),
    )
    return jax.shard_map(
        body,
        mesh=mesh,
        in_specs=placed,
        out_specs=(
            P(("fsdp", "tp"), None),
            P(("fsdp", "tp"), None),
            P(None, "fsdp"),
            P(None, None, "fsdp", "tp"),
            P(None, "tp", "fsdp"),
            P(None, "fsdp"),
            P("fsdp", "tp"),
            P("tp", "fsdp"),
            P("fsdp", None),
            P(None, "fsdp", "tp"),
            P(None, "tp", "fsdp"),
        ),
        check_vma=False,
    )
```

```python
import functools
import itertools

import jax
import jax.numpy as jnp
from jax import lax
from jax.experimental import pallas as pl
from jax.experimental.pallas import tpu as pltpu
from jax.sharding import PartitionSpec as P

HEAD = 64
SEQ = 197
D = 768
HALF = 1536
SMALL = 128
WIDE = HALF + SMALL
MESH = pl.DeviceIdType.MESH
GROUPS = [[4 * k + j for j in range(4)] for k in range(16)]

epsilon = 1e-06
precise = lax.Precision.HIGHEST

ORDERS = (("x", "y", "z"), ("y", "z", "x"), ("z", "x", "y"))
BOTH = 2 * HALF
ALL = WIDE + BOTH
SET_AT = (0, 512, 896, 1280)
SMALL_AT = 384
CHUNK = 384
TILE = 512
EARLY = 1536
SLOTS = 4
SETS = 4
PASS = 768


def to_low(values):
    return values.astype(jnp.bfloat16)


def coordinates():
    f, t = lax.axis_index("fsdp"), lax.axis_index("tp")
    return {
        "x": lax.rem(lax.div(f, 8), 4),
        "y": 2 * t + lax.div(f, 32),
        "z": lax.rem(lax.div(f, 2), 4),
        "c": lax.rem(f, 2),
    }


def device_at(place):
    y = place["y"]
    f = ((lax.rem(y, 2) * 4 + place["x"]) * 4 + place["z"]) * 2 + place["c"]
    return (f, lax.div(y, 2))


def moved(place, axis, steps):
    return {**place, axis: lax.rem(place[axis] + steps + 4, 4)}


def greet(place):
    others = [device_at(moved(place, a, s)) for a in "xyz" for s in (1, -1)]
    others.append(device_at({**place, "c": 1 - place["c"]}))
    barrier = pltpu.get_barrier_semaphore()
    for other in others:
        pl.semaphore_signal(barrier, inc=1, device_id=other, device_id_type=MESH)
    pl.semaphore_wait(barrier, len(others))


def cube(where, whole):
    every = slice(None)
    y = (every, every) if "y" in whole else (lax.div(where["y"], 2), lax.rem(where["y"], 2))
    z = (every, every) if "z" in whole else (lax.rem(where["z"], 2), lax.div(where["z"], 2))
    x = every if "x" in whole else where["x"]
    return (z[0], y[0], y[1], x, z[1])


def halves(width):
    first = (width // 256) * 128
    if width - first > first:
        first = width - first
    return (slice(0, first), slice(first, width))


def remote(src, dst, send, recv, target):
    return pltpu.make_async_remote_copy(
        src_ref=src,
        dst_ref=dst,
        send_sem=send,
        recv_sem=recv,
        device_id=device_at(target),
        device_id_type=MESH,
    )


class Gather:
    def __init__(self, me, shard, whole, spans, sems):
        self.me, self.items = me, [(shard, whole, span) for span in spans]
        self.send, self.recv, self.send_pair, self.recv_pair, self.own = sems
        self.sibling = {**me, "c": 1 - me["c"]}

    def block(self, i, p, where, whole, cols):
        z_lo, t, y_lo, x, z_hi = cube(where, whole)
        rows = pl.ds(16 * p, 16)
        return self.items[i][1].at[z_lo, self.me["c"], t, y_lo, x, z_hi, rows, cols]

    def mine(self, i):
        z_lo, t, y_lo, x, z_hi = cube(self.me, ())
        return self.items[i][1].at[z_lo, self.me["c"], t, y_lo, x, z_hi, :, self.items[i][2]]

    def own_copy(self, i):
        shard, _, cols = self.items[i]
        return pltpu.make_async_copy(shard.at[:, cols], self.mine(i), self.own.at[i])

    def hop(self, i, p, phase, kind):
        axis, done = ORDERS[p][phase], ORDERS[p][:phase]
        cols = self.items[i][2]
        step = 1 if kind % 2 == 0 else -1
        if kind < 2:
            dst = self.block(i, p, self.me, done, cols)
            src = dst
            if phase == 0:
                src = self.items[i][0].at[pl.ds(16 * p, 16), cols]
        else:
            part = halves(cols.stop - cols.start)[kind - 2]
            span = slice(cols.start + part.start, cols.start + part.stop)
            src = dst = self.block(i, p, moved(self.me, axis, -step), done, span)
        send, recv = self.send.at[i, p, phase, kind], self.recv.at[i, p, phase, kind]
        return remote(src, dst, send, recv, moved(self.me, axis, step))

    def across(self, i, slot):
        send, recv = self.send_pair.at[i, slot], self.recv_pair.at[i, slot]
        shard, _, cols = self.items[i]
        if slot == 0:
            return remote(shard.at[:, cols], self.mine(i), send, recv, self.sibling)
        phase, p, which = (slot - 1) // 9, (slot - 1) // 3 % 3, (slot - 1) % 3
        axis, done = ORDERS[p][phase], ORDERS[p][:phase]
        part = self.block(i, p, moved(self.me, axis, (-1, 1, 2)[which]), done, cols)
        return remote(part, part, send, recv, self.sibling)

    def advance(self, i, stage):
        if stage == 0:
            self.own_copy(i).start()
            self.across(i, 0).start()
        phase, late = divmod(stage, 2)
        if late == 0:
            if phase > 0:
                for p in range(3):
                    for kind in (2, 3):
                        self.hop(i, p, phase - 1, kind).wait_recv()
                    if phase < 3:
                        for kind in (0, 1):
                            if phase == 1 and p == 0 and kind == 0:
                                self.own_copy(i).wait()
                            self.hop(i, p, phase, kind).start()
                    self.across(i, 9 * (phase - 1) + 3 * p + 3).start()
            else:
                for p in range(3):
                    for kind in (0, 1):
                        self.hop(i, p, 0, kind).start()
        else:
            for p in range(3):
                for kind in (0, 1):
                    self.hop(i, p, phase, kind).wait_recv()
                    self.hop(i, p, phase, 2 + kind).start()
                for which in (0, 1):
                    self.across(i, 9 * phase + 3 * p + 1 + which).start()

    def arrived(self, i):
        for slot in range(28):
            self.across(i, slot).wait_recv()

    def drain(self, i):
        for p in range(3):
            for phase in range(3):
                for kind in range(4):
                    self.hop(i, p, phase, kind).wait_send()
        for slot in range(28):
            self.across(i, slot).wait_send()


def gather_sems(n):
    dma = pltpu.SemaphoreType.DMA
    return [dma((n, 3, 3, 4)), dma((n, 3, 3, 4)), dma((n, 28)), dma((n, 28)), dma((n,))]


def lead_of(whole):
    dims = []
    if "z" in whole:
        dims.append(2)
    if "y" in whole:
        dims += [2, 2]
    if "x" in whole:
        dims.append(4)
    if "z" in whole:
        dims.append(2)
    return tuple(dims)


def split_index(i, dims):
    out = []
    for size in reversed(dims):
        out.append(lax.rem(i, size))
        i = lax.div(i, size)
    return tuple(reversed(out))


def with_index(where, whole, index):
    rest = list(index)
    full = list(cube(where, whole))
    for place, value in enumerate(full):
        if isinstance(value, slice):
            full[place] = rest.pop(0)
    return tuple(full)


RS_ORDERS = tuple(tuple(reversed(order)) for order in ORDERS)


class Reduce:
    def __init__(self, me, passes, held, boxes, stage, sems):
        self.me, self.passes = me, passes
        self.widths = [passed[1].stop - passed[1].start for passed in passes]
        self.held = [held[m % SETS].at[..., 0:w] for m, w in enumerate(self.widths)]
        self.all_boxes, self.stage = boxes, stage
        self.send, self.recv, self.own_sem, self.stage_sem, self.free_sem = sems

    def box(self, m, p, phase, kind):
        w = self.widths[m]
        if kind < 2:
            part = halves(w)[kind]
            w = part.stop - part.start
        return self.all_boxes[m % SETS, p, phase][kind].at[..., 0:w]

    def own_copy(self, m):
        own, span = self.passes[m][:2]
        src = own.at[:, :, :, :, :, :, span]
        return pltpu.make_async_copy(src, self.held[m], self.own_sem.at[m])

    def begin(self, m):
        self.own_copy(m).start()

    def neighbours(self):
        return [device_at(moved(self.me, axis, step)) for axis in "xyz" for step in (1, -1)]

    def stage_copy(self, m, i, slot):
        z_lo, t, y_lo = split_index(i, (2, 2, 2))
        return pltpu.make_async_copy(
            self.passes[m][2].at[z_lo, t, y_lo, :, :, :, self.passes[m][3]],
            self.stage.at[slot, :, :, :, pl.ds(0, self.widths[m])],
            self.stage_sem.at[slot],
        )

    def add_pair(self, m):
        held, stage = self.held[m], self.stage
        self.stage_copy(m, 0, 0).start()
        self.stage_copy(m, 1, 1).start()
        self.own_copy(m).wait()

        @pl.loop(0, 8)
        def _(i):
            slot = lax.rem(i, 3)

            @pl.when(i < 6)
            def _():
                self.stage_copy(m, i + 2, lax.rem(i + 2, 3)).start()

            self.stage_copy(m, i, slot).wait()
            z_lo, t, y_lo = split_index(i, (2, 2, 2))

            @pl.loop(0, 4)
            def _(x):
                for z_hi in range(2):
                    for r in range(0, 48, 16):
                        place = (z_lo, t, y_lo, x, z_hi, pl.ds(r, 16), slice(None))
                        other = stage[slot, x, z_hi, pl.ds(r, 16), pl.ds(0, self.widths[m])]
                        held[place] = held[place] + other

    def exchange(self, m, p, phase, kind):
        axis, whole = RS_ORDERS[p][phase], RS_ORDERS[p][phase + 1 :]
        step = 1 if kind % 2 == 0 else -1
        if kind < 2:
            source = moved(self.me, axis, 2)
            span = halves(self.widths[m])[kind]
        else:
            source = moved(self.me, axis, step)
            span = slice(None)
        return remote(
            self.held[m].at[(*cube(source, whole), pl.ds(16 * p, 16), span)],
            self.box(m, p, phase, kind),
            self.send.at[m, p, phase, kind],
            self.recv.at[m, p, phase, kind],
            moved(self.me, axis, step),
        )

    def add_boxes(self, m, p, phase, where, span, kinds):
        whole = RS_ORDERS[p][phase + 1 :]
        dims = lead_of(whole)
        count = 1
        for size in dims:
            count *= size
        held = self.held[m]

        @pl.loop(0, count)
        def _(i):
            index = split_index(i, dims)
            place = (*with_index(where, whole, index), pl.ds(16 * p, 16), span)
            if len(kinds) == 1:
                held[place] = held[place] + self.box(m, p, phase, kinds[0])[index]
            else:
                total = held[place].astype(jnp.float32)
                for kind in kinds:
                    total = total + self.box(m, p, phase, kind)[index].astype(jnp.float32)
                held[place] = to_low(total)

    def run(self, m, stage_number):
        if stage_number == 0:
            self.add_pair(m)
            if m >= SETS:
                pl.semaphore_wait(self.free_sem.at[m % SETS], 6)
            for p in range(3):
                for kind in (0, 1):
                    self.exchange(m, p, 0, kind).start()
            return
        me = self.me
        phase, late = divmod(stage_number - 1, 2)
        for p in range(3):
            axis = RS_ORDERS[p][phase]
            if late == 0:
                for kind, step in ((0, 1), (1, -1)):
                    self.exchange(m, p, phase, kind).wait_recv()
                    span = halves(self.widths[m])[kind]
                    self.add_boxes(m, p, phase, moved(me, axis, step), span, (kind,))
                    self.exchange(m, p, phase, 2 + kind).start()
            else:
                for kind in (2, 3):
                    self.exchange(m, p, phase, kind).wait_recv()
                self.add_boxes(m, p, phase, me, slice(None), (2, 3))
                if phase < 2:
                    for kind in (0, 1):
                        self.exchange(m, p, phase + 1, kind).start()
                else:
                    rows = pl.ds(16 * p, 16)
                    sums, span = self.passes[m][4:]
                    sums[rows, span] = self.held[m][(*cube(me, ()), rows, slice(None))]
        if stage_number == 6:
            for p in range(3):
                for phase in range(3):
                    for kind in range(4):
                        self.exchange(m, p, phase, kind).wait_send()
            if m + SETS < len(self.passes):
                for other in self.neighbours():
                    pl.semaphore_signal(
                        self.free_sem.at[m % SETS], inc=1, device_id=other, device_id_type=MESH
                    )


def reduce_scratch(count):
    shapes = []
    w = PASS
    for _ in range(SETS):
        shapes.append(pltpu.VMEM((2, 2, 2, 4, 2, 48, w), jnp.bfloat16))
        for p in range(3):
            for phase in range(3):
                lead = lead_of(RS_ORDERS[p][phase + 1 :])
                for width in (w // 2, w // 2, w, w):
                    shapes.append(pltpu.VMEM((*lead, 16, width), jnp.bfloat16))
    dma = pltpu.SemaphoreType.DMA
    shapes += [
        pltpu.VMEM((3, 4, 2, 48, w), jnp.bfloat16),
        dma((count, 3, 3, 4)),
        dma((count, 3, 3, 4)),
        dma((count,)),
        dma((3,)),
        pltpu.SemaphoreType.REGULAR((SETS,)),
    ]
    return shapes


def make_reduce(me, passes, refs):
    refs = list(refs)
    held, boxes = [], {}
    for m in range(SETS):
        held.append(refs.pop(0))
        for p in range(3):
            for phase in range(3):
                boxes[m, p, phase] = [refs.pop(0) for _ in range(4)]
    return Reduce(me, passes, held, boxes, refs[0], refs[1:])


def cut_up(widths):
    starts = [sum(widths[:i]) for i in range(len(widths))]
    return [slice(a, a + w) for a, w in zip(starts, widths)]


PAD = 208
SCALE = HEAD ** (-0.5)
FWD_LOADS = ((0, 0), (0, 1), (1, 0), (2, 0), (1, 1), (2, 1), (3, 0), (3, 1))
BWD_LOADS = ((3, 0), (3, 1), (1, 0), (2, 0), (1, 1), (2, 1), (0, 0), (0, 1))


def cols_of(ref, cols):
    if len(ref.shape) == 2:
        return ref[:, cols]
    return ref[:, :, :, :, cols].reshape(D, -1)


def put_cols(ref, cols, value):
    ref[:, :, :, :, cols] = to_low(value).reshape(2, 4, 2, 48, value.shape[1])


def nn(a, b):
    return lax.dot_general(a, b, (((1,), (0,)), ((), ())), preferred_element_type=jnp.float32)


def nt(a, b):
    return lax.dot_general(a, b, (((1,), (1,)), ((), ())), preferred_element_type=jnp.float32)


def turned(values):
    return to_low(jnp.transpose(values.astype(jnp.float32)))


def norm_parts(s):
    centre = s - jnp.mean(s, axis=-1, keepdims=True)
    r = lax.rsqrt(jnp.mean(centre * centre, axis=-1, keepdims=True) + epsilon)
    return centre * r, r


def norm_low(s, gain):
    return to_low(norm_parts(s)[0] * gain)


def norm_pull(s, gain, in_grad):
    xhat, r = norm_parts(s)
    u = in_grad * gain
    first = jnp.mean(u, axis=-1, keepdims=True)
    second = jnp.mean(u * xhat, axis=-1, keepdims=True)
    return r * (u - first - xhat * second), jnp.sum(xhat * in_grad, axis=0, keepdims=True)


def normal_cdf(x):
    return 0.5 * (1.0 + lax.erf(x * 0.7071067811865476))


def gelu_slope(x, cdf):
    return cdf + x * (0.3989422804014327 * jnp.exp(-0.5 * x * x))


def head_masks():
    lane = lax.broadcasted_iota(jnp.int32, (PAD, 128), 1)
    return lane < HEAD, lane >= HEAD


def probabilities(q, k):
    scores = nt(q, k) * SCALE
    key = lax.broadcasted_iota(jnp.int32, scores.shape, 1)
    scores = jnp.where(key < SEQ, scores, -1e30)
    scores = jnp.exp(scores - jnp.max(scores, axis=-1, keepdims=True))
    return scores / jnp.sum(scores, axis=-1, keepdims=True)


def lanes(start):
    return pl.ds(pl.multiple_of(start, 128), 128)


def attend_forward(res, gain, weight, x_s, qkv, mixed, out):
    x_s[...] = norm_low(res[...], gain)
    x = x_s[...]
    for t in range(2):
        qkv[t, :, :] = to_low(nn(x, cols_of(weight[t], slice(0, 1152))))
        yield
    for t in range(2):

        @pl.loop(0, 3)
        def _(pair):
            at = pair * 128
            q, k, v = [qkv[t, :, lanes(at + 384 * j)] for j in range(3)]
            parts = []
            for mask in head_masks():
                probs = probabilities(jnp.where(mask, q, jnp.zeros_like(q)), k)
                parts.append(nn(to_low(probs), v))
            mixed[t, :, lanes(at)] = to_low(jnp.where(head_masks()[0], parts[0], parts[1]))

        yield
    total = res[...]
    for t in range(2):
        total = total + nt(mixed[t], cols_of(weight[t], slice(1152, HALF)))
    out[...] = total
    yield


def dense_forward(res, gain, up, down, x_s, out, t):
    if t == 0:
        x_s[...] = norm_low(res[...], gain)
        out[...] = res[...]
    for j in range(0, HALF, 512):
        cols = slice(j, j + 512)
        pre = nn(x_s[...], cols_of(up, cols))
        act = to_low(pre * normal_cdf(pre))
        out[...] += nt(act, cols_of(down, cols))
        yield


def hidden_tile(x, x_t, g, g_t, up, down, put_up, put_down):
    pre = nn(x, up)
    cdf = normal_cdf(pre)
    act = to_low(pre * cdf)
    pre_grad = to_low(gelu_slope(pre, cdf) * nn(g, down))
    put_down(to_low(nn(g_t, act)))
    put_up(to_low(nn(x_t, pre_grad)))
    return nt(act, down), nt(pre_grad, up)


def experts_kernel(*refs):
    (act_in, cot_in, chosen, shard) = refs[:4]
    (whole, own, landed, result, stream, r1, r2) = refs[4:11]
    (qkv0, qkv1, mixed0, mixed1, gain_out, router_out) = refs[11:17]
    (w, res, x_s, x_t, bg, og, og_t, branch, din, cgrad, e_w, e_g, w_sem, small_s) = refs[17:31]
    small_sem, e_sem, g_sem, put_sem, got_sem = refs[31:36]
    me = coordinates()
    greet(me)
    sibling = {**me, "c": 1 - me["c"]}
    work = Gather(me, shard, whole, cut_up((512, 768, 384, 1024, 1024, 1024)), refs[36:])

    def load(n, q):
        s, t = FWD_LOADS[n]
        cols = slice(SET_AT[s], SET_AT[s] + CHUNK)
        return pltpu.make_async_copy(
            whole.at[q // 2, q % 2, t, :, :, :, :, cols],
            w.at[n % 4, :, :, :, :, CHUNK * q : CHUNK * q + CHUNK],
            w_sem.at[n, q],
        )

    def load_start(*numbers):
        for n in numbers:
            for q in range(4):
                load(n, q).start()

    def load_wait(*numbers):
        for n in numbers:
            for q in range(4):
                load(n, q).wait()

    for event in FIRST_EVENTS:
        work.advance(*event)
    bg[...] = jnp.zeros((PAD, D), jnp.bfloat16)
    bg[0:SEQ, :] = cot_in[...]
    res[...] = jnp.zeros((PAD, D), jnp.float32)
    res[0:SEQ, :] = act_in[...].astype(jnp.float32)
    work.arrived(0)
    load_start(0, 1)
    small_copy = pltpu.make_async_copy(
        whole.at[0, 0, 0, :, :, :, :, pl.ds(SMALL_AT, SMALL)], small_s, small_sem.at[0]
    )
    small_copy.start()
    small_copy.wait()
    small = small_s[...].reshape(D, SMALL)
    rows = jnp.transpose(small.astype(jnp.float32))
    gains = [rows[j : j + 1, :] for j in range(4)]

    def forward():
        load_wait(0, 1)
        yield from attend_forward(res, gains[0], [w.at[0], w.at[1]], x_s, qkv0, mixed0, r1)
        load_start(4, 5)
        for t in range(2):
            load_wait(2 + 2 * t, 3 + 2 * t)
            up, down = (w.at[2], w.at[3]) if t == 0 else (w.at[0], w.at[1])
            yield from dense_forward(r1, gains[2], up, down, x_s, r2, t)
            if t == 0:
                load_start(6, 7)
        load_wait(6, 7)
        yield from attend_forward(r2, gains[1], [w.at[2], w.at[3]], x_s, qkv1, mixed1, res)

    for n, _ in enumerate(forward()):
        for item, stage in FORWARD_EVENTS.get(n + 1, ()):
            if stage < 7:
                work.advance(item, stage)
            else:
                work.arrived(item)
                if item == 1:
                    load_start(2, 3)

    x_s[...] = norm_low(res[...], gains[3])
    x_t[...] = turned(x_s[...])
    lane = lax.broadcasted_iota(jnp.int32, (PAD, 128), 1)
    logits = nn(x_s[...], small)
    logits = jnp.where((lane >= 4) & (lane < 8), logits, -1e30)
    probs = jnp.exp(logits - jnp.max(logits, axis=-1, keepdims=True))
    probs = probs / jnp.sum(probs, axis=-1, keepdims=True)
    combine = probs * chosen[...]
    branch[...] = res[...]
    din[...] = jnp.zeros((PAD, D), jnp.float32)
    cgrad[...] = jnp.zeros((PAD, 128), jnp.float32)
    for e in range(4):
        gated = combine[:, 4 + e : 5 + e] * bg[...].astype(jnp.float32)
        og[e] = to_low(gated)
        og_t[e] = turned(to_low(gated))

    def place(i):
        h, e, t = split_index(i, (3, 4, 2))
        return h, e, t, lax.div(e, 2), lax.rem(e, 2)

    def fetch(i):
        h, e, t, z_lo, c = place(i)
        cols = pl.ds(pl.multiple_of(WIDE + h * 2 * TILE, 128), 2 * TILE)
        slot = lax.rem(i, SLOTS)
        return [
            pltpu.make_async_copy(
                whole.at[z_lo, c, t, y_lo, :, :, :, cols], e_w.at[slot, y_lo], e_sem.at[slot, y_lo]
            )
            for y_lo in range(2)
        ]

    def fetch_start(i):
        for copy in fetch(i):
            copy.start()

    def store(i):
        h, e, t, z_lo, c = place(i)
        slot = lax.rem(i, SLOTS)
        copies = []
        for part in range(2):
            cols = pl.ds(pl.multiple_of(h * 2 * TILE + part * TILE, 128), TILE)
            copies.append(
                pltpu.make_async_copy(
                    e_g.at[slot, part], own.at[z_lo, c, t, :, cols], g_sem.at[slot, part]
                )
            )
        return copies

    def early_pair(z_lo):
        cols = slice(0, EARLY)
        return remote(
            own.at[z_lo, 1 - me["c"], :, :, cols],
            landed.at[z_lo, :, :, cols],
            put_sem.at[z_lo],
            got_sem.at[z_lo],
            sibling,
        )

    @pl.loop(0, 24)
    def _(i):
        slot = lax.rem(i, SLOTS)
        for turn, events in LOOP_EVENTS.items():

            @pl.when(i == turn)
            def _():
                for item, stage in events:
                    if stage < 7:
                        work.advance(item, stage)
                    else:
                        work.arrived(item)

        @pl.when(lax.rem(i, 8) == 0)
        def _():
            for ahead in range(SLOTS - 1):
                fetch_start(i + ahead)

        @pl.when(lax.rem(i, 8) < 9 - SLOTS)
        def _():
            fetch_start(i + SLOTS - 1)

        for copy in fetch(i):
            copy.wait()

        @pl.when(i >= SLOTS)
        def _():
            for copy in store(i - SLOTS):
                copy.wait()

        h, e, t, _, _ = place(i)
        out = jnp.zeros((PAD, D), jnp.float32)
        back = jnp.zeros((PAD, D), jnp.float32)
        for j in range(0, TILE, 256):

            def put(part, value, j=j):
                e_g[slot, part, :, j : j + 256] = value

            up = e_w[slot, :, :, :, :, j : j + 256].reshape(D, 256)
            down = e_w[slot, :, :, :, :, TILE + j : TILE + j + 256].reshape(D, 256)
            a, b = hidden_tile(
                x_s[...], x_t[...], og[e], og_t[e], up, down,
                functools.partial(put, 0), functools.partial(put, 1),
            )
            out, back = out + a, back + b
        for copy in store(i):
            copy.start()

        @pl.when(i == 16 + SLOTS)
        def _():
            early_pair(0).start()
            early_pair(1).start()

        mine = lane == 4 + e
        gate = jnp.sum(jnp.where(mine, combine, 0.0), axis=-1, keepdims=True)
        branch[...] += gate * out
        din[...] += back
        share = jnp.sum(out * bg[...].astype(jnp.float32), axis=-1, keepdims=True)
        cgrad[...] += jnp.where(mine, share, 0.0)

    result[...] = to_low(branch[0:SEQ, :])
    probs_grad = cgrad[...] * chosen[...]
    logit_grad = probs * (probs_grad - jnp.sum(probs * probs_grad, axis=-1, keepdims=True))
    high = to_low(logit_grad)
    rest = to_low(logit_grad - high.astype(jnp.float32))
    router_out[...] = nn(x_t[...], high) + nn(x_t[...], rest)
    in_grad = din[...] + nt(high, small) + nt(rest, small)
    back, gain_grad = norm_pull(res[...], gains[3], in_grad)
    gain_out[...] = gain_grad
    stream[...] = bg[...].astype(jnp.float32) + back
    for i in range(24 - SLOTS, 24):
        for copy in store(i):
            copy.wait()
    for z_lo in range(2):
        early_pair(z_lo).wait()
    for i in range(6):
        work.drain(i)


FIRST_EVENTS = ((0, 0), (1, 0), (2, 0), (3, 0), (4, 0), (5, 0), (0, 1), (1, 1), (2, 1), (3, 1), (4, 1), (5, 1), (0, 2), (1, 2), (2, 2), (3, 2), (0, 3), (1, 3), (2, 3), (4, 2), (3, 3), (0, 4), (4, 3), (1, 4), (0, 5), (2, 4), (1, 5), (0, 6),)
FORWARD_EVENTS = {
    1: ((2, 5),),
    3: ((3, 4),),
    4: ((1, 6), (1, 7),),
    5: ((2, 6), (2, 7),),
    12: ((4, 4),),
    15: ((3, 5),),
}
LOOP_EVENTS = {
    0: ((4, 5), (3, 6), (3, 7), (5, 2),),
    2: ((5, 3),),
    3: ((5, 4),),
    4: ((4, 6),),
    8: ((4, 7),),
    11: ((5, 5),),
    16: ((5, 6), (5, 7),),
}


def run_experts(activations, cotangent, chosen, shard):
    f32, bf16 = jnp.float32, jnp.bfloat16
    shape = jax.ShapeDtypeStruct
    vmem, hbm = pl.BlockSpec(memory_space=pltpu.VMEM), pl.BlockSpec(memory_space=pl.ANY)
    dma = pltpu.SemaphoreType.DMA
    return pl.pallas_call(
        experts_kernel,
        out_shape=[
            shape((2, 2, 2, 2, 4, 2, 48, ALL), bf16),
            shape((2, 2, 2, D, BOTH), bf16),
            shape((2, 2, D, BOTH), bf16),
            shape((SEQ, D), bf16),
            shape((PAD, D), f32),
            shape((PAD, D), f32),
            shape((PAD, D), f32),
            shape((2, PAD, 1152), bf16),
            shape((2, PAD, 1152), bf16),
            shape((2, PAD, 384), bf16),
            shape((2, PAD, 384), bf16),
            shape((1, D), f32),
            shape((D, 128), f32),
        ],
        in_specs=[vmem, vmem, vmem, hbm],
        out_specs=[hbm] * 3 + [vmem] * 10,
        scratch_shapes=[
            pltpu.VMEM((4, 2, 4, 2, 48, HALF), bf16),
            pltpu.VMEM((PAD, D), f32),
            pltpu.VMEM((PAD, D), bf16),
            pltpu.VMEM((D, PAD), bf16),
            pltpu.VMEM((PAD, D), bf16),
            pltpu.VMEM((4, PAD, D), bf16),
            pltpu.VMEM((4, D, PAD), bf16),
            pltpu.VMEM((PAD, D), f32),
            pltpu.VMEM((PAD, D), f32),
            pltpu.VMEM((PAD, 128), f32),
            pltpu.VMEM((SLOTS, 2, 4, 2, 48, 2 * TILE), bf16),
            pltpu.VMEM((SLOTS, 2, D, TILE), bf16),
            dma((8, 4)),
            pltpu.VMEM((2, 4, 2, 48, SMALL), bf16),
            dma((1,)),
            dma((SLOTS, 2)),
            dma((SLOTS, 2)),
            dma((2,)),
            dma((2,)),
            *gather_sems(6),
        ],
        compiler_params=pltpu.CompilerParams(
            collective_id=1, has_side_effects=True, vmem_limit_bytes=60 * 1024 * 1024
        ),
        name="forward_experts",
    )(activations, cotangent, chosen, shard)


def attend_backward(stream, res, gain, weight, qkv, mixed, s, tools, put_gain):
    x_s, x_t, bg, bg_t, din, dmix, dqkv, grad_slot, grad_send = tools
    bg[...] = to_low(stream[...])
    bg_t[...] = turned(bg[...])
    x_s[...] = norm_low(res[...].astype(jnp.float32), gain)
    x_t[...] = turned(x_s[...])
    yield
    for t in range(2):
        dmix[...] = to_low(nn(bg[...], weight[t][:, 1152:HALF]))

        @pl.loop(0, 3)
        def _(pair):
            at = pair * 128
            q, k, v = [qkv[t, :, lanes(at + 384 * j)] for j in range(3)]
            m = dmix[:, lanes(at)]
            parts = []
            for mask in head_masks():
                probs = probabilities(jnp.where(mask, q, jnp.zeros_like(q)), k)
                prob_grad = nt(jnp.where(mask, m, jnp.zeros_like(m)), v)
                inner = jnp.sum(probs * prob_grad, axis=-1, keepdims=True)
                score_grad = probs * (prob_grad - inner)
                v_grad = nn(turned(to_low(probs)), m)
                q_grad = nn(to_low(score_grad), k) * SCALE
                k_grad = nn(turned(to_low(score_grad)), q) * SCALE
                parts.append((q_grad, k_grad, v_grad))
            for j in range(3):
                both = jnp.where(head_masks()[0], parts[0][j], parts[1][j])
                dqkv[:, lanes(at + 384 * j)] = to_low(both)

        yield
        slot = grad_slot(s, t)
        put_cols(slot, slice(1152, HALF), nn(bg_t[...], mixed[t]))
        for j in range(0, 1152, 384):
            put_cols(slot, slice(j, j + 384), nn(x_t[...], dqkv[:, j : j + 384]))
        grad_send(s, t)
        part = nt(dqkv[...], weight[t][:, :1152])
        if t == 0:
            din[...] = part
        else:
            din[...] += part
        yield
    back, gain_grad = norm_pull(res[...].astype(jnp.float32), gain, din[...])
    stream[...] += back
    put_gain(gain_grad)
    yield


def dense_backward(stream, res, gain, up, down, t, tools, put_gain):
    x_s, x_t, bg, bg_t, din, dmix, dqkv, grad_slot, grad_send = tools
    if t == 0:
        bg[...] = to_low(stream[...])
        bg_t[...] = turned(bg[...])
        x_s[...] = norm_low(res[...], gain)
        x_t[...] = turned(x_s[...])
        din[...] = jnp.zeros((PAD, D), jnp.float32)
        yield
    slots = grad_slot(1, t), grad_slot(2, t)

    @pl.loop(0, 3)
    def _(n):
        back = jnp.zeros((PAD, D), jnp.float32)
        for half in range(2):
            cols = pl.ds(pl.multiple_of(n * 512 + 256 * half, 128), 256)
            pre = nn(x_s[...], up[:, cols])
            cdf = normal_cdf(pre)
            act = to_low(pre * cdf)
            pre_grad = to_low(gelu_slope(pre, cdf) * nn(bg[...], down[:, cols]))
            put_cols(slots[0], cols, nn(x_t[...], pre_grad))
            put_cols(slots[1], cols, nn(bg_t[...], act))
            back = back + nt(pre_grad, up[:, cols])
        din[...] += back

    grad_send(1, t)
    grad_send(2, t)
    yield
    if t == 1:
        back, gain_grad = norm_pull(res[...], gain, din[...])
        stream[...] += back
        put_gain(gain_grad)
        yield


PASS_COUNT = 7
YIELDS = 16
PASS_EVENTS = {
    0: ((0, 0), (1, 0), (2, 0), (3, 0),),
    1: ((0, 1),),
    2: ((1, 1),),
    3: ((2, 1),),
    4: ((3, 1),),
    6: ((0, 2),),
    8: ((1, 2),),
    11: ((2, 2),),
    13: ((0, 3), (3, 2), (1, 3), (2, 3),),
    14: ((0, 4), (3, 3), (1, 4),),
    15: ((0, 5), (3, 4), (1, 5), (2, 4), (0, 6), (3, 5), (1, 6), (2, 5), (4, 0), (3, 6), (5, 0), (2, 6), (4, 1),),
    17: ((6, 0), (5, 1), (4, 2), (6, 1), (5, 2), (4, 3), (6, 2), (5, 3), (4, 4), (6, 3), (5, 4), (4, 5), (6, 4), (5, 5), (4, 6), (6, 5), (5, 6), (6, 6),),
}


def backward_kernel(*refs):
    (act_in, base, stream_in, r1, r2) = refs[:5]
    (qkv0, qkv1, mixed0, mixed1, gain_in, router_in, grad_e, land_e) = refs[5:13]
    (own, landed, late, stream_out, sum_all) = refs[13:18]
    (w, g, stream, res0, x_s, x_t, bg, bg_t, din, dmix, dqkv, rows_s, small_s, tail_s) = refs[18:32]
    w_sem, keep_sem, put_sem, got_sem, small_sem, late_send, late_recv = refs[32:39]
    me = coordinates()
    greet(me)
    sibling = {**me, "c": 1 - me["c"]}
    mine_e = grad_e.at[:, me["c"]]
    passes = [
        (
            mine_e,
            slice(768 * n, 768 * n + 768),
            land_e if n < 2 else late.at[n - 2],
            slice(768 * n, 768 * n + 768) if n < 2 else slice(0, 768),
            sum_all,
            slice(WIDE + 768 * n, WIDE + 768 * n + 768),
        )
        for n in range(4)
    ]
    for a, b in ((1280, 1664), (512, 1280), (0, 512)):
        passes.append((own, slice(a, b), landed, slice(a, b), sum_all, slice(a, b)))
    work = make_reduce(me, passes, refs[39:])

    def late_copy(n, z_lo):
        cols = slice(EARLY + 768 * n, EARLY + 768 * n + 768)
        return remote(
            grad_e.at[z_lo, 1 - me["c"], :, :, :, :, :, cols],
            late.at[n, z_lo],
            late_send.at[n, z_lo],
            late_recv.at[n, z_lo],
            sibling,
        )

    def load_parts(n):
        s, t = BWD_LOADS[n]
        cols = slice(SET_AT[s], SET_AT[s] + CHUNK)
        return [
            pltpu.make_async_copy(
                base.at[q, t, :, cols],
                w.at[n % 3, :, CHUNK * q : CHUNK * q + CHUNK],
                w_sem.at[n, q],
            )
            for q in range(4)
        ]

    def load_start(*numbers):
        for n in numbers:
            for copy in load_parts(n):
                copy.start()

    def load_wait(*numbers):
        for n in numbers:
            for copy in load_parts(n):
                copy.wait()

    work.begin(0)
    load_start(0, 1, 2)
    for n in range(2):
        for z_lo in range(2):
            late_copy(n, z_lo).start()
    work.begin(1)
    work.begin(2)
    work.begin(3)
    small_copy = pltpu.make_async_copy(
        base.at[0, 0, :, pl.ds(SMALL_AT, SMALL)], small_s, small_sem.at[0]
    )
    small_copy.start()
    stream[...] = stream_in[...]
    res0[...] = jnp.zeros((PAD, D), jnp.bfloat16)
    res0[0:SEQ, :] = act_in[...]
    small_copy.wait()
    turned_small = jnp.transpose(small_s[...].astype(jnp.float32))
    gains = [turned_small[j : j + 1, :] for j in range(4)]
    rows_s[...] = jnp.zeros((128, D), jnp.float32)
    rows_s[3:4, :] = gain_in[...]

    def pieces(n):
        s, t = BWD_LOADS[n]
        cols = slice(SET_AT[s], SET_AT[s] + CHUNK)
        copies = []
        for z_lo in range(2):
            at = [
                pl.ds(pl.multiple_of(CHUNK * (2 * z_lo + c), 128), CHUNK)
                for c in (me["c"], 1 - me["c"])
            ]
            keep = pltpu.make_async_copy(
                g.at[n % 2, :, :, :, :, at[0]],
                own.at[z_lo, t, :, :, :, :, cols],
                keep_sem.at[n, z_lo],
            )
            give = remote(
                g.at[n % 2, :, :, :, :, at[1]],
                landed.at[z_lo, t, :, :, :, :, cols],
                put_sem.at[n, z_lo],
                got_sem.at[n, z_lo],
                sibling,
            )
            copies.append((keep, give))
        return copies

    waited = set()

    def send_wait(n):
        if n in waited:
            return
        waited.add(n)
        for keep, give in pieces(n):
            keep.wait()
            give.wait_send()

    def grad_slot(s, t):
        n = BWD_LOADS.index((s, t))
        if n >= 2:
            send_wait(n - 2)
        return g.at[n % 2]

    def grad_send(s, t):
        for keep, give in pieces(BWD_LOADS.index((s, t))):
            keep.start()
            give.start()

    tools = (x_s, x_t, bg, bg_t, din, dmix, dqkv, grad_slot, grad_send)

    def put_gain(j, value):
        rows_s[j : j + 1, :] = value

    def backward():
        load_wait(0, 1)
        yield from attend_backward(
            stream, r2, gains[1], [w.at[0], w.at[1]], qkv1, mixed1, 3, tools,
            functools.partial(put_gain, 1),
        )
        load_start(3, 4)
        load_wait(2, 3)
        put = functools.partial(put_gain, 2)
        yield from dense_backward(stream, r1, gains[2], w.at[2], w.at[0], 0, tools, put)
        load_start(5, 6)
        load_wait(4, 5)
        yield from dense_backward(stream, r1, gains[2], w.at[1], w.at[2], 1, tools, put)
        load_start(7)
        load_wait(6, 7)
        yield from attend_backward(
            stream, res0, gains[0], [w.at[0], w.at[1]], qkv0, mixed0, 0, tools,
            functools.partial(put_gain, 0),
        )

    tails = []
    made_of = {4: (0, 1), 5: (2, 3, 4, 5), 6: (6, 7)}

    def run_events(turn):
        for m, stage in plan.get(turn, ()):
            if stage == 0 and m in (2, 3):
                for z_lo in range(2):
                    late_copy(m - 2, z_lo).wait()
            if stage == 0 and m in made_of:
                for n in made_of[m]:
                    send_wait(n)
                    for _, give in pieces(n):
                        give.wait_recv()
                if m == 6:
                    for keep, give in tails:
                        keep.wait()
                        give.wait()
                work.begin(m)
            work.run(m, stage)

    plan = PASS_EVENTS
    run_events(0)
    for n, _ in enumerate(backward()):
        run_events(n + 1)
    tail_s[...] = to_low(jnp.transpose(rows_s[...]) + router_in[...]).reshape(tail_s.shape)
    for n in range(4):
        place = (n // 2, n % 2, *[slice(None)] * 4, slice(SMALL_AT, SMALL_AT + SMALL))
        keep = pltpu.make_async_copy(tail_s, own.at[place], keep_sem.at[8, n])
        give = remote(tail_s, landed.at[place], put_sem.at[8, n], got_sem.at[8, n], sibling)
        keep.start()
        give.start()
        tails.append((keep, give))
    stream_out[...] = stream[0:SEQ, :]
    run_events(YIELDS + 1)


def run_backward(*args):
    f32, bf16 = jnp.float32, jnp.bfloat16
    shape = jax.ShapeDtypeStruct
    vmem, hbm = pl.BlockSpec(memory_space=pltpu.VMEM), pl.BlockSpec(memory_space=pl.ANY)
    dma = pltpu.SemaphoreType.DMA
    blocks = (2, 2, 2, 4, 2, 48, WIDE)
    cubes = [args[-2].reshape(2, 2, 2, 2, 4, 2, 48, BOTH), args[-1].reshape(2, 2, 2, 4, 2, 48, BOTH)]
    return pl.pallas_call(
        backward_kernel,
        out_shape=[
            shape(blocks, bf16),
            shape(blocks, bf16),
            shape((2, 2, 2, 2, 4, 2, 48, PASS), bf16),
            shape((SEQ, D), f32),
            shape((48, ALL), bf16),
        ],
        in_specs=[vmem, hbm] + [vmem] * 9 + [hbm] * 2,
        out_specs=[hbm, hbm, hbm, vmem, vmem],
        scratch_shapes=[
            pltpu.VMEM((3, D, HALF), bf16),
            pltpu.VMEM((2, 2, 4, 2, 48, HALF), bf16),
            pltpu.VMEM((PAD, D), f32),
            pltpu.VMEM((PAD, D), bf16),
            pltpu.VMEM((PAD, D), bf16),
            pltpu.VMEM((D, PAD), bf16),
            pltpu.VMEM((PAD, D), bf16),
            pltpu.VMEM((D, PAD), bf16),
            pltpu.VMEM((PAD, D), f32),
            pltpu.VMEM((PAD, 384), bf16),
            pltpu.VMEM((PAD, 1152), bf16),
            pltpu.VMEM((128, D), f32),
            pltpu.VMEM((D, 128), bf16),
            pltpu.VMEM((2, 4, 2, 48, 128), bf16),
            dma((8, 4)),
            dma((9, 4)),
            dma((9, 4)),
            dma((9, 4)),
            dma((1,)),
            dma((2, 2)),
            dma((2, 2)),
            *reduce_scratch(PASS_COUNT),
        ],
        compiler_params=pltpu.CompilerParams(
            collective_id=2, has_side_effects=True, vmem_limit_bytes=62 * 1024 * 1024
        ),
        name="backward_reduce",
    )(*args[:-2], *cubes)


def body(
    activations,
    attn_gain,
    qkv_weight,
    out_weight,
    ffn_gain,
    mlp_up,
    mlp_down,
    router,
    expert_up,
    expert_down,
    routes,
    cotangent,
):
    small = jnp.concatenate([attn_gain.T, ffn_gain.T, router], axis=1)
    small = jnp.pad(small, ((0, 0), (0, SMALL - 8)))
    out_t = jnp.transpose(out_weight, (0, 2, 1))
    attn = [jnp.concatenate([qkv_weight[b], out_t[b][None]], axis=0) for b in range(2)]

    def chunks(matrix):
        return jnp.transpose(matrix.reshape(12, 4, CHUNK), (1, 0, 2))

    pair = jnp.stack(
        [
            expert_up.reshape(4, 12, 3, TILE),
            jnp.transpose(expert_down, (0, 2, 1)).reshape(4, 12, 3, TILE),
        ],
        axis=3,
    ).reshape(4, 12, BOTH)
    sets = jnp.concatenate(
        [
            attn[0],
            jnp.broadcast_to(small, (4, *small.shape)),
            chunks(mlp_up),
            chunks(mlp_down.T),
            attn[1],
            pair,
        ],
        axis=2,
    )
    sets = lax.all_to_all(
        sets, "fsdp", split_axis=0, concat_axis=0, tiled=True, axis_index_groups=GROUPS
    )
    shard = sets.reshape(48, ALL)
    half = lax.axis_index("tp")
    my_routes = lax.dynamic_slice_in_dim(routes, half * SEQ, SEQ, 0)
    labels = jnp.arange(-4, 124, dtype=jnp.int32)
    chosen = jnp.sum((my_routes[:, :, None] == labels).astype(jnp.float32), axis=1)
    chosen = jnp.pad(chosen, ((0, PAD - SEQ), (0, 0)))
    outs = run_experts(activations, cotangent, chosen, shard)
    whole, grad_e, land_e, result, stream, r1, r2 = outs[:7]
    qkv0, qkv1, mixed0, mixed1, gain_grad, router_grad = outs[7:]
    _, _, _, stream, sums = run_backward(
        activations, whole.reshape(4, 2, D, ALL), stream, r1, r2, qkv0, qkv1, mixed0, mixed1,
        gain_grad, router_grad, grad_e, land_e,
    )
    sums = sums.reshape(4, 12, ALL)
    sums = lax.all_to_all(
        sums, "fsdp", split_axis=0, concat_axis=0, tiled=True, axis_index_groups=GROUPS
    ).astype(jnp.float32)
    first, up, down, second = [sums[:, :, at : at + CHUNK] for at in SET_AT]
    tail = sums[0, :, SMALL_AT : SMALL_AT + SMALL]
    pair = sums[:, :, WIDE:].reshape(4, 12, 3, 2, TILE)
    return (
        result,
        stream,
        tail[:, 0:2].T,
        jnp.stack([first[:3], second[:3]]),
        jnp.stack([first[3].T, second[3].T]),
        tail[:, 2:4].T,
        jnp.transpose(up, (1, 0, 2)).reshape(12, HALF),
        jnp.transpose(down, (0, 2, 1)).reshape(HALF, 12),
        tail[:, 4:8],
        pair[:, :, :, 0].reshape(4, 12, HALF),
        jnp.transpose(pair[:, :, :, 1].reshape(4, 12, HALF), (0, 2, 1)),
    )


def solution(mesh):
    placed = (
        P(("fsdp", "tp"), None),
        P(None, "fsdp"),
        P(None, None, "fsdp", "tp"),
        P(None, "tp", "fsdp"),
        P(None, "fsdp"),
        P("fsdp", "tp"),
        P("tp", "fsdp"),
        P("fsdp", None),
        P(None, "fsdp", "tp"),
        P(None, "tp", "fsdp"),
        P("fsdp", None),
        P(("fsdp", "tp"), None),
    )
    return jax.shard_map(
        body,
        mesh=mesh,
        in_specs=placed,
        out_specs=(
            P(("fsdp", "tp"), None),
            P(("fsdp", "tp"), None),
            P(None, "fsdp"),
            P(None, None, "fsdp", "tp"),
            P(None, "tp", "fsdp"),
            P(None, "fsdp"),
            P("fsdp", "tp"),
            P("tp", "fsdp"),
            P("fsdp", None),
            P(None, "fsdp", "tp"),
            P(None, "tp", "fsdp"),
        ),
        check_vma=False,
    )
```

```python
import functools
import itertools

import jax
import jax.numpy as jnp
from jax import lax
from jax.experimental import pallas as pl
from jax.experimental.pallas import tpu as pltpu
from jax.sharding import PartitionSpec as P

HEAD = 64
SEQ = 197
D = 768
HALF = 1536
SMALL = 128
WIDE = HALF + SMALL
MESH = pl.DeviceIdType.MESH
GROUPS = [[4 * k + j for j in range(4)] for k in range(16)]

epsilon = 1e-06
precise = lax.Precision.HIGHEST

ORDERS = (("x", "y", "z"), ("y", "z", "x"), ("z", "x", "y"))
BOTH = 2 * HALF
ALL = WIDE + BOTH
SET_AT = (0, 512, 896, 1280)
SMALL_AT = 384
CHUNK = 384
TILE = 512
EARLY = 1536
SLOTS = 4
SETS = 4
PASS = 768


def to_low(values):
    return values.astype(jnp.bfloat16)


def coordinates():
    f, t = lax.axis_index("fsdp"), lax.axis_index("tp")
    return {
        "x": lax.rem(lax.div(f, 8), 4),
        "y": 2 * t + lax.div(f, 32),
        "z": lax.rem(lax.div(f, 2), 4),
        "c": lax.rem(f, 2),
    }


def device_at(place):
    y = place["y"]
    f = ((lax.rem(y, 2) * 4 + place["x"]) * 4 + place["z"]) * 2 + place["c"]
    return (f, lax.div(y, 2))


def moved(place, axis, steps):
    return {**place, axis: lax.rem(place[axis] + steps + 4, 4)}


def greet(place):
    others = [device_at(moved(place, a, s)) for a in "xyz" for s in (1, -1)]
    others.append(device_at({**place, "c": 1 - place["c"]}))
    barrier = pltpu.get_barrier_semaphore()
    for other in others:
        pl.semaphore_signal(barrier, inc=1, device_id=other, device_id_type=MESH)
    pl.semaphore_wait(barrier, len(others))


def cube(where, whole):
    every = slice(None)
    y = (every, every) if "y" in whole else (lax.div(where["y"], 2), lax.rem(where["y"], 2))
    z = (every, every) if "z" in whole else (lax.rem(where["z"], 2), lax.div(where["z"], 2))
    x = every if "x" in whole else where["x"]
    return (z[0], y[0], y[1], x, z[1])


def halves(width):
    first = (width // 256) * 128
    if width - first > first:
        first = width - first
    return (slice(0, first), slice(first, width))


def remote(src, dst, send, recv, target):
    return pltpu.make_async_remote_copy(
        src_ref=src,
        dst_ref=dst,
        send_sem=send,
        recv_sem=recv,
        device_id=device_at(target),
        device_id_type=MESH,
    )


class Gather:
    def __init__(self, me, shard, whole, spans, sems):
        self.me, self.items = me, [(shard, whole, span) for span in spans]
        self.send, self.recv, self.send_pair, self.recv_pair, self.own = sems
        self.sibling = {**me, "c": 1 - me["c"]}

    def block(self, i, p, where, whole, cols):
        z_lo, t, y_lo, x, z_hi = cube(where, whole)
        rows = pl.ds(16 * p, 16)
        return self.items[i][1].at[z_lo, self.me["c"], t, y_lo, x, z_hi, rows, cols]

    def mine(self, i):
        z_lo, t, y_lo, x, z_hi = cube(self.me, ())
        return self.items[i][1].at[z_lo, self.me["c"], t, y_lo, x, z_hi, :, self.items[i][2]]

    def own_copy(self, i):
        shard, _, cols = self.items[i]
        return pltpu.make_async_copy(shard.at[:, cols], self.mine(i), self.own.at[i])

    def hop(self, i, p, phase, kind):
        axis, done = ORDERS[p][phase], ORDERS[p][:phase]
        cols = self.items[i][2]
        step = 1 if kind % 2 == 0 else -1
        if kind < 2:
            dst = self.block(i, p, self.me, done, cols)
            src = dst
            if phase == 0:
                src = self.items[i][0].at[pl.ds(16 * p, 16), cols]
        else:
            part = halves(cols.stop - cols.start)[kind - 2]
            span = slice(cols.start + part.start, cols.start + part.stop)
            src = dst = self.block(i, p, moved(self.me, axis, -step), done, span)
        send, recv = self.send.at[i, p, phase, kind], self.recv.at[i, p, phase, kind]
        return remote(src, dst, send, recv, moved(self.me, axis, step))

    def across(self, i, slot):
        send, recv = self.send_pair.at[i, slot], self.recv_pair.at[i, slot]
        shard, _, cols = self.items[i]
        if slot == 0:
            return remote(shard.at[:, cols], self.mine(i), send, recv, self.sibling)
        phase, p, which = (slot - 1) // 9, (slot - 1) // 3 % 3, (slot - 1) % 3
        axis, done = ORDERS[p][phase], ORDERS[p][:phase]
        part = self.block(i, p, moved(self.me, axis, (-1, 1, 2)[which]), done, cols)
        return remote(part, part, send, recv, self.sibling)

    def advance(self, i, stage):
        if stage == 0:
            self.own_copy(i).start()
            self.across(i, 0).start()
        phase, late = divmod(stage, 2)
        if late == 0:
            if phase > 0:
                for p in range(3):
                    for kind in (2, 3):
                        self.hop(i, p, phase - 1, kind).wait_recv()
                    if phase < 3:
                        for kind in (0, 1):
                            if phase == 1 and p == 0 and kind == 0:
                                self.own_copy(i).wait()
                            self.hop(i, p, phase, kind).start()
                    self.across(i, 9 * (phase - 1) + 3 * p + 3).start()
            else:
                for p in range(3):
                    for kind in (0, 1):
                        self.hop(i, p, 0, kind).start()
        else:
            for p in range(3):
                for kind in (0, 1):
                    self.hop(i, p, phase, kind).wait_recv()
                    self.hop(i, p, phase, 2 + kind).start()
                for which in (0, 1):
                    self.across(i, 9 * phase + 3 * p + 1 + which).start()

    def arrived(self, i):
        for slot in range(28):
            self.across(i, slot).wait_recv()

    def drain(self, i):
        for p in range(3):
            for phase in range(3):
                for kind in range(4):
                    self.hop(i, p, phase, kind).wait_send()
        for slot in range(28):
            self.across(i, slot).wait_send()


def gather_sems(n):
    dma = pltpu.SemaphoreType.DMA
    return [dma((n, 3, 3, 4)), dma((n, 3, 3, 4)), dma((n, 28)), dma((n, 28)), dma((n,))]


def lead_of(whole):
    dims = []
    if "z" in whole:
        dims.append(2)
    if "y" in whole:
        dims += [2, 2]
    if "x" in whole:
        dims.append(4)
    if "z" in whole:
        dims.append(2)
    return tuple(dims)


def split_index(i, dims):
    out = []
    for size in reversed(dims):
        out.append(lax.rem(i, size))
        i = lax.div(i, size)
    return tuple(reversed(out))


def with_index(where, whole, index):
    rest = list(index)
    full = list(cube(where, whole))
    for place, value in enumerate(full):
        if isinstance(value, slice):
            full[place] = rest.pop(0)
    return tuple(full)


RS_ORDERS = tuple(tuple(reversed(order)) for order in ORDERS)


class Reduce:
    def __init__(self, me, passes, held, boxes, stage, sems):
        self.me, self.passes = me, passes
        self.widths = [passed[1].stop - passed[1].start for passed in passes]
        self.held = [held[m % SETS].at[..., 0:w] for m, w in enumerate(self.widths)]
        self.all_boxes, self.stage = boxes, stage
        self.send, self.recv, self.own_sem, self.stage_sem, self.free_sem = sems

    def box(self, m, p, phase, kind):
        w = self.widths[m]
        if kind < 2:
            part = halves(w)[kind]
            w = part.stop - part.start
        return self.all_boxes[m % SETS, p, phase][kind].at[..., 0:w]

    def own_copy(self, m):
        own, span = self.passes[m][:2]
        src = own.at[:, :, :, :, :, :, span]
        return pltpu.make_async_copy(src, self.held[m], self.own_sem.at[m])

    def begin(self, m):
        self.own_copy(m).start()

    def neighbours(self):
        return [device_at(moved(self.me, axis, step)) for axis in "xyz" for step in (1, -1)]

    def stage_copy(self, m, i, slot):
        z_lo, t, y_lo = split_index(i, (2, 2, 2))
        return pltpu.make_async_copy(
            self.passes[m][2].at[z_lo, t, y_lo, :, :, :, self.passes[m][3]],
            self.stage.at[slot, :, :, :, pl.ds(0, self.widths[m])],
            self.stage_sem.at[slot],
        )

    def add_pair(self, m):
        held, stage = self.held[m], self.stage
        self.stage_copy(m, 0, 0).start()
        self.stage_copy(m, 1, 1).start()
        self.own_copy(m).wait()

        @pl.loop(0, 8)
        def _(i):
            slot = lax.rem(i, 3)

            @pl.when(i < 6)
            def _():
                self.stage_copy(m, i + 2, lax.rem(i + 2, 3)).start()

            self.stage_copy(m, i, slot).wait()
            z_lo, t, y_lo = split_index(i, (2, 2, 2))

            @pl.loop(0, 4)
            def _(x):
                for z_hi in range(2):
                    for r in range(0, 48, 16):
                        place = (z_lo, t, y_lo, x, z_hi, pl.ds(r, 16), slice(None))
                        other = stage[slot, x, z_hi, pl.ds(r, 16), pl.ds(0, self.widths[m])]
                        held[place] = held[place] + other

    def exchange(self, m, p, phase, kind):
        axis, whole = RS_ORDERS[p][phase], RS_ORDERS[p][phase + 1 :]
        step = 1 if kind % 2 == 0 else -1
        if kind < 2:
            source = moved(self.me, axis, 2)
            span = halves(self.widths[m])[kind]
        else:
            source = moved(self.me, axis, step)
            span = slice(None)
        return remote(
            self.held[m].at[(*cube(source, whole), pl.ds(16 * p, 16), span)],
            self.box(m, p, phase, kind),
            self.send.at[m, p, phase, kind],
            self.recv.at[m, p, phase, kind],
            moved(self.me, axis, step),
        )

    def add_boxes(self, m, p, phase, where, span, kinds):
        whole = RS_ORDERS[p][phase + 1 :]
        dims = lead_of(whole)
        count = 1
        for size in dims:
            count *= size
        held = self.held[m]

        @pl.loop(0, count)
        def _(i):
            index = split_index(i, dims)
            place = (*with_index(where, whole, index), pl.ds(16 * p, 16), span)
            if len(kinds) == 1:
                held[place] = held[place] + self.box(m, p, phase, kinds[0])[index]
            else:
                total = held[place].astype(jnp.float32)
                for kind in kinds:
                    total = total + self.box(m, p, phase, kind)[index].astype(jnp.float32)
                held[place] = to_low(total)

    def run(self, m, stage_number):
        if stage_number == 0:
            self.add_pair(m)
            if m >= SETS:
                pl.semaphore_wait(self.free_sem.at[m % SETS], 6)
            for p in range(3):
                for kind in (0, 1):
                    self.exchange(m, p, 0, kind).start()
            return
        me = self.me
        phase, late = divmod(stage_number - 1, 2)
        for p in range(3):
            axis = RS_ORDERS[p][phase]
            if late == 0:
                for kind, step in ((0, 1), (1, -1)):
                    self.exchange(m, p, phase, kind).wait_recv()
                    span = halves(self.widths[m])[kind]
                    self.add_boxes(m, p, phase, moved(me, axis, step), span, (kind,))
                    self.exchange(m, p, phase, 2 + kind).start()
            else:
                for kind in (2, 3):
                    self.exchange(m, p, phase, kind).wait_recv()
                self.add_boxes(m, p, phase, me, slice(None), (2, 3))
                if phase < 2:
                    for kind in (0, 1):
                        self.exchange(m, p, phase + 1, kind).start()
                else:
                    rows = pl.ds(16 * p, 16)
                    sums, span = self.passes[m][4:]
                    sums[rows, span] = self.held[m][(*cube(me, ()), rows, slice(None))]
        if stage_number == 6:
            for p in range(3):
                for phase in range(3):
                    for kind in range(4):
                        self.exchange(m, p, phase, kind).wait_send()
            if m + SETS < len(self.passes):
                for other in self.neighbours():
                    pl.semaphore_signal(
                        self.free_sem.at[m % SETS], inc=1, device_id=other, device_id_type=MESH
                    )


def reduce_scratch(count):
    shapes = []
    w = PASS
    for _ in range(SETS):
        shapes.append(pltpu.VMEM((2, 2, 2, 4, 2, 48, w), jnp.bfloat16))
        for p in range(3):
            for phase in range(3):
                lead = lead_of(RS_ORDERS[p][phase + 1 :])
                for width in (w // 2, w // 2, w, w):
                    shapes.append(pltpu.VMEM((*lead, 16, width), jnp.bfloat16))
    dma = pltpu.SemaphoreType.DMA
    shapes += [
        pltpu.VMEM((3, 4, 2, 48, w), jnp.bfloat16),
        dma((count, 3, 3, 4)),
        dma((count, 3, 3, 4)),
        dma((count,)),
        dma((3,)),
        pltpu.SemaphoreType.REGULAR((SETS,)),
    ]
    return shapes


def make_reduce(me, passes, refs):
    refs = list(refs)
    held, boxes = [], {}
    for m in range(SETS):
        held.append(refs.pop(0))
        for p in range(3):
            for phase in range(3):
                boxes[m, p, phase] = [refs.pop(0) for _ in range(4)]
    return Reduce(me, passes, held, boxes, refs[0], refs[1:])


def cut_up(widths):
    starts = [sum(widths[:i]) for i in range(len(widths))]
    return [slice(a, a + w) for a, w in zip(starts, widths)]


PAD = 208
SCALE = HEAD ** (-0.5)
FWD_LOADS = ((0, 0), (0, 1), (1, 0), (2, 0), (1, 1), (2, 1), (3, 0), (3, 1))
BWD_LOADS = ((3, 0), (3, 1), (1, 0), (2, 0), (1, 1), (2, 1), (0, 0), (0, 1))


def cols_of(ref, cols):
    if len(ref.shape) == 2:
        return ref[:, cols]
    return ref[:, :, :, :, cols].reshape(D, -1)


def put_cols(ref, cols, value):
    ref[:, :, :, :, cols] = to_low(value).reshape(2, 4, 2, 48, value.shape[1])


def nn(a, b):
    return lax.dot_general(a, b, (((1,), (0,)), ((), ())), preferred_element_type=jnp.float32)


def nt(a, b):
    return lax.dot_general(a, b, (((1,), (1,)), ((), ())), preferred_element_type=jnp.float32)


def turned(values):
    return to_low(jnp.transpose(values.astype(jnp.float32)))


def norm_parts(s):
    centre = s - jnp.mean(s, axis=-1, keepdims=True)
    r = lax.rsqrt(jnp.mean(centre * centre, axis=-1, keepdims=True) + epsilon)
    return centre * r, r


def norm_low(s, gain):
    return to_low(norm_parts(s)[0] * gain)


def norm_pull(s, gain, in_grad):
    xhat, r = norm_parts(s)
    u = in_grad * gain
    first = jnp.mean(u, axis=-1, keepdims=True)
    second = jnp.mean(u * xhat, axis=-1, keepdims=True)
    return r * (u - first - xhat * second), jnp.sum(xhat * in_grad, axis=0, keepdims=True)


def normal_cdf(x):
    return 0.5 * (1.0 + lax.erf(x * 0.7071067811865476))


def gelu_slope(x, cdf):
    return cdf + x * (0.3989422804014327 * jnp.exp(-0.5 * x * x))


def head_masks():
    lane = lax.broadcasted_iota(jnp.int32, (PAD, 128), 1)
    return lane < HEAD, lane >= HEAD


def probabilities(q, k):
    scores = nt(q, k) * SCALE
    key = lax.broadcasted_iota(jnp.int32, scores.shape, 1)
    scores = jnp.where(key < SEQ, scores, -1e30)
    scores = jnp.exp(scores - jnp.max(scores, axis=-1, keepdims=True))
    return scores / jnp.sum(scores, axis=-1, keepdims=True)


def lanes(start):
    return pl.ds(pl.multiple_of(start, 128), 128)


def attend_forward(res, gain, weight, x_s, qkv, mixed, out):
    x_s[...] = norm_low(res[...], gain)
    x = x_s[...]
    for t in range(2):
        qkv[t, :, :] = to_low(nn(x, cols_of(weight[t], slice(0, 1152))))
        yield
    for t in range(2):

        @pl.loop(0, 3)
        def _(pair):
            at = pair * 128
            q, k, v = [qkv[t, :, lanes(at + 384 * j)] for j in range(3)]
            parts = []
            for mask in head_masks():
                probs = probabilities(jnp.where(mask, q, jnp.zeros_like(q)), k)
                parts.append(nn(to_low(probs), v))
            mixed[t, :, lanes(at)] = to_low(jnp.where(head_masks()[0], parts[0], parts[1]))

        yield
    total = res[...]
    for t in range(2):
        total = total + nt(mixed[t], cols_of(weight[t], slice(1152, HALF)))
    out[...] = total
    yield


def dense_forward(res, gain, up, down, x_s, out, t):
    if t == 0:
        x_s[...] = norm_low(res[...], gain)
        out[...] = res[...]
    for j in range(0, HALF, 512):
        cols = slice(j, j + 512)
        pre = nn(x_s[...], cols_of(up, cols))
        act = to_low(pre * normal_cdf(pre))
        out[...] += nt(act, cols_of(down, cols))
        yield


def hidden_tile(x, x_t, g, g_t, up, down, put_up, put_down):
    pre = nn(x, up)
    cdf = normal_cdf(pre)
    act = to_low(pre * cdf)
    pre_grad = to_low(gelu_slope(pre, cdf) * nn(g, down))
    put_down(to_low(nn(g_t, act)))
    put_up(to_low(nn(x_t, pre_grad)))
    return nt(act, down), nt(pre_grad, up)


def experts_kernel(*refs):
    (act_in, cot_in, chosen, shard) = refs[:4]
    (whole, own, landed, result, stream, r1, r2) = refs[4:11]
    (qkv0, qkv1, mixed0, mixed1, gain_out, router_out) = refs[11:17]
    (w, res, x_s, x_t, bg, og, og_t, branch, din, cgrad, e_w, e_g, w_sem, small_s) = refs[17:31]
    small_sem, e_sem, g_sem, put_sem, got_sem = refs[31:36]
    me = coordinates()
    greet(me)
    sibling = {**me, "c": 1 - me["c"]}
    work = Gather(me, shard, whole, cut_up((512, 768, 384, 1024, 1024, 1024)), refs[36:])

    def load(n, q):
        s, t = FWD_LOADS[n]
        cols = slice(SET_AT[s], SET_AT[s] + CHUNK)
        return pltpu.make_async_copy(
            whole.at[q // 2, q % 2, t, :, :, :, :, cols],
            w.at[n % 4, :, :, :, :, CHUNK * q : CHUNK * q + CHUNK],
            w_sem.at[n, q],
        )

    def load_start(*numbers):
        for n in numbers:
            for q in range(4):
                load(n, q).start()

    def load_wait(*numbers):
        for n in numbers:
            for q in range(4):
                load(n, q).wait()

    for event in FIRST_EVENTS:
        work.advance(*event)
    bg[...] = jnp.zeros((PAD, D), jnp.bfloat16)
    bg[0:SEQ, :] = cot_in[...]
    res[...] = jnp.zeros((PAD, D), jnp.float32)
    res[0:SEQ, :] = act_in[...].astype(jnp.float32)
    work.arrived(0)
    load_start(0, 1)
    small_copy = pltpu.make_async_copy(
        whole.at[0, 0, 0, :, :, :, :, pl.ds(SMALL_AT, SMALL)], small_s, small_sem.at[0]
    )
    small_copy.start()
    small_copy.wait()
    small = small_s[...].reshape(D, SMALL)
    rows = jnp.transpose(small.astype(jnp.float32))
    gains = [rows[j : j + 1, :] for j in range(4)]

    def forward():
        load_wait(0, 1)
        yield from attend_forward(res, gains[0], [w.at[0], w.at[1]], x_s, qkv0, mixed0, r1)
        load_start(4, 5)
        for t in range(2):
            load_wait(2 + 2 * t, 3 + 2 * t)
            up, down = (w.at[2], w.at[3]) if t == 0 else (w.at[0], w.at[1])
            yield from dense_forward(r1, gains[2], up, down, x_s, r2, t)
            if t == 0:
                load_start(6, 7)
        load_wait(6, 7)
        yield from attend_forward(r2, gains[1], [w.at[2], w.at[3]], x_s, qkv1, mixed1, res)

    for n, _ in enumerate(forward()):
        for item, stage in FORWARD_EVENTS.get(n + 1, ()):
            if stage < 7:
                work.advance(item, stage)
            else:
                work.arrived(item)
                if item == 1:
                    load_start(2, 3)

    x_s[...] = norm_low(res[...], gains[3])
    x_t[...] = turned(x_s[...])
    lane = lax.broadcasted_iota(jnp.int32, (PAD, 128), 1)
    logits = nn(x_s[...], small)
    logits = jnp.where((lane >= 4) & (lane < 8), logits, -1e30)
    probs = jnp.exp(logits - jnp.max(logits, axis=-1, keepdims=True))
    probs = probs / jnp.sum(probs, axis=-1, keepdims=True)
    combine = probs * chosen[...]
    branch[...] = res[...]
    din[...] = jnp.zeros((PAD, D), jnp.float32)
    cgrad[...] = jnp.zeros((PAD, 128), jnp.float32)
    for e in range(4):
        gated = combine[:, 4 + e : 5 + e] * bg[...].astype(jnp.float32)
        og[e] = to_low(gated)
        og_t[e] = turned(to_low(gated))

    def place(i):
        h, e, t = split_index(i, (3, 4, 2))
        return h, e, t, lax.div(e, 2), lax.rem(e, 2)

    def fetch(i):
        h, e, t, z_lo, c = place(i)
        cols = pl.ds(pl.multiple_of(WIDE + h * 2 * TILE, 128), 2 * TILE)
        slot = lax.rem(i, SLOTS)
        return [
            pltpu.make_async_copy(
                whole.at[z_lo, c, t, y_lo, :, :, :, cols], e_w.at[slot, y_lo], e_sem.at[slot, y_lo]
            )
            for y_lo in range(2)
        ]

    def fetch_start(i):
        for copy in fetch(i):
            copy.start()

    def store(i):
        h, e, t, z_lo, c = place(i)
        slot = lax.rem(i, SLOTS)
        copies = []
        for part in range(2):
            cols = pl.ds(pl.multiple_of(h * 2 * TILE + part * TILE, 128), TILE)
            copies.append(
                pltpu.make_async_copy(
                    e_g.at[slot, part], own.at[z_lo, c, t, :, cols], g_sem.at[slot, part]
                )
            )
        return copies

    def early_pair(z_lo):
        cols = slice(0, EARLY)
        return remote(
            own.at[z_lo, 1 - me["c"], :, :, cols],
            landed.at[z_lo, :, :, cols],
            put_sem.at[z_lo],
            got_sem.at[z_lo],
            sibling,
        )

    @pl.loop(0, 24)
    def _(i):
        slot = lax.rem(i, SLOTS)
        for turn, events in LOOP_EVENTS.items():

            @pl.when(i == turn)
            def _():
                for item, stage in events:
                    if stage < 7:
                        work.advance(item, stage)
                    else:
                        work.arrived(item)

        @pl.when(lax.rem(i, 8) == 0)
        def _():
            for ahead in range(SLOTS - 1):
                fetch_start(i + ahead)

        @pl.when(lax.rem(i, 8) < 9 - SLOTS)
        def _():
            fetch_start(i + SLOTS - 1)

        for copy in fetch(i):
            copy.wait()

        @pl.when(i >= SLOTS)
        def _():
            for copy in store(i - SLOTS):
                copy.wait()

        h, e, t, _, _ = place(i)
        out = jnp.zeros((PAD, D), jnp.float32)
        back = jnp.zeros((PAD, D), jnp.float32)
        for j in range(0, TILE, 256):

            def put(part, value, j=j):
                e_g[slot, part, :, j : j + 256] = value

            up = e_w[slot, :, :, :, :, j : j + 256].reshape(D, 256)
            down = e_w[slot, :, :, :, :, TILE + j : TILE + j + 256].reshape(D, 256)
            a, b = hidden_tile(
                x_s[...], x_t[...], og[e], og_t[e], up, down,
                functools.partial(put, 0), functools.partial(put, 1),
            )
            out, back = out + a, back + b
        for copy in store(i):
            copy.start()

        @pl.when(i == 16 + SLOTS)
        def _():
            early_pair(0).start()
            early_pair(1).start()

        mine = lane == 4 + e
        gate = jnp.sum(jnp.where(mine, combine, 0.0), axis=-1, keepdims=True)
        branch[...] += gate * out
        din[...] += back
        share = jnp.sum(out * bg[...].astype(jnp.float32), axis=-1, keepdims=True)
        cgrad[...] += jnp.where(mine, share, 0.0)

    result[...] = to_low(branch[0:SEQ, :])
    probs_grad = cgrad[...] * chosen[...]
    logit_grad = probs * (probs_grad - jnp.sum(probs * probs_grad, axis=-1, keepdims=True))
    high = to_low(logit_grad)
    rest = to_low(logit_grad - high.astype(jnp.float32))
    router_out[...] = nn(x_t[...], high) + nn(x_t[...], rest)
    in_grad = din[...] + nt(high, small) + nt(rest, small)
    back, gain_grad = norm_pull(res[...], gains[3], in_grad)
    gain_out[...] = gain_grad
    stream[...] = bg[...].astype(jnp.float32) + back
    for i in range(24 - SLOTS, 24):
        for copy in store(i):
            copy.wait()
    for z_lo in range(2):
        early_pair(z_lo).wait()
    for i in range(6):
        work.drain(i)


FIRST_EVENTS = (
    *((item, stage) for stage in range(4) for item in range(6)),
    (0, 4), (1, 4), (2, 4), (0, 5), (3, 4), (1, 5), (2, 5), (0, 6),
)
FORWARD_EVENTS = {
    1: ((4, 4),),
    3: ((1, 6), (1, 7),),
    5: ((2, 6), (2, 7),),
    10: ((3, 5),),
    12: ((5, 4),),
}
LOOP_EVENTS = {
    0: ((3, 6), (3, 7),),
    1: ((4, 5),),
    4: ((4, 6),),
    8: ((4, 7), (5, 5),),
    12: ((5, 6),),
    16: ((5, 7),),
}


def run_experts(activations, cotangent, chosen, shard):
    f32, bf16 = jnp.float32, jnp.bfloat16
    shape = jax.ShapeDtypeStruct
    vmem, hbm = pl.BlockSpec(memory_space=pltpu.VMEM), pl.BlockSpec(memory_space=pl.ANY)
    dma = pltpu.SemaphoreType.DMA
    return pl.pallas_call(
        experts_kernel,
        out_shape=[
            shape((2, 2, 2, 2, 4, 2, 48, ALL), bf16),
            shape((2, 2, 2, D, BOTH), bf16),
            shape((2, 2, D, BOTH), bf16),
            shape((SEQ, D), bf16),
            shape((PAD, D), f32),
            shape((PAD, D), f32),
            shape((PAD, D), f32),
            shape((2, PAD, 1152), bf16),
            shape((2, PAD, 1152), bf16),
            shape((2, PAD, 384), bf16),
            shape((2, PAD, 384), bf16),
            shape((1, D), f32),
            shape((D, 128), f32),
        ],
        in_specs=[vmem, vmem, vmem, hbm],
        out_specs=[hbm] * 3 + [vmem] * 10,
        scratch_shapes=[
            pltpu.VMEM((4, 2, 4, 2, 48, HALF), bf16),
            pltpu.VMEM((PAD, D), f32),
            pltpu.VMEM((PAD, D), bf16),
            pltpu.VMEM((D, PAD), bf16),
            pltpu.VMEM((PAD, D), bf16),
            pltpu.VMEM((4, PAD, D), bf16),
            pltpu.VMEM((4, D, PAD), bf16),
            pltpu.VMEM((PAD, D), f32),
            pltpu.VMEM((PAD, D), f32),
            pltpu.VMEM((PAD, 128), f32),
            pltpu.VMEM((SLOTS, 2, 4, 2, 48, 2 * TILE), bf16),
            pltpu.VMEM((SLOTS, 2, D, TILE), bf16),
            dma((8, 4)),
            pltpu.VMEM((2, 4, 2, 48, SMALL), bf16),
            dma((1,)),
            dma((SLOTS, 2)),
            dma((SLOTS, 2)),
            dma((2,)),
            dma((2,)),
            *gather_sems(6),
        ],
        compiler_params=pltpu.CompilerParams(
            collective_id=1, has_side_effects=True, vmem_limit_bytes=60 * 1024 * 1024
        ),
        name="forward_experts",
    )(activations, cotangent, chosen, shard)


def attend_backward(stream, res, gain, weight, qkv, mixed, s, tools, put_gain):
    x_s, x_t, bg, bg_t, din, dmix, dqkv, grad_slot, grad_send = tools
    bg[...] = to_low(stream[...])
    bg_t[...] = turned(bg[...])
    x_s[...] = norm_low(res[...].astype(jnp.float32), gain)
    x_t[...] = turned(x_s[...])
    yield
    for t in range(2):
        dmix[...] = to_low(nn(bg[...], weight[t][:, 1152:HALF]))

        @pl.loop(0, 3)
        def _(pair):
            at = pair * 128
            q, k, v = [qkv[t, :, lanes(at + 384 * j)] for j in range(3)]
            m = dmix[:, lanes(at)]
            parts = []
            for mask in head_masks():
                probs = probabilities(jnp.where(mask, q, jnp.zeros_like(q)), k)
                prob_grad = nt(jnp.where(mask, m, jnp.zeros_like(m)), v)
                inner = jnp.sum(probs * prob_grad, axis=-1, keepdims=True)
                score_grad = probs * (prob_grad - inner)
                v_grad = nn(turned(to_low(probs)), m)
                q_grad = nn(to_low(score_grad), k) * SCALE
                k_grad = nn(turned(to_low(score_grad)), q) * SCALE
                parts.append((q_grad, k_grad, v_grad))
            for j in range(3):
                both = jnp.where(head_masks()[0], parts[0][j], parts[1][j])
                dqkv[:, lanes(at + 384 * j)] = to_low(both)

        yield
        slot = grad_slot(s, t)
        put_cols(slot, slice(1152, HALF), nn(bg_t[...], mixed[t]))
        for j in range(0, 1152, 384):
            put_cols(slot, slice(j, j + 384), nn(x_t[...], dqkv[:, j : j + 384]))
        grad_send(s, t)
        part = nt(dqkv[...], weight[t][:, :1152])
        if t == 0:
            din[...] = part
        else:
            din[...] += part
        yield
    back, gain_grad = norm_pull(res[...].astype(jnp.float32), gain, din[...])
    stream[...] += back
    put_gain(gain_grad)
    yield


def dense_backward(stream, res, gain, up, down, t, tools, put_gain):
    x_s, x_t, bg, bg_t, din, dmix, dqkv, grad_slot, grad_send = tools
    if t == 0:
        bg[...] = to_low(stream[...])
        bg_t[...] = turned(bg[...])
        x_s[...] = norm_low(res[...], gain)
        x_t[...] = turned(x_s[...])
        din[...] = jnp.zeros((PAD, D), jnp.float32)
        yield
    slots = grad_slot(1, t), grad_slot(2, t)

    @pl.loop(0, 3)
    def _(n):
        back = jnp.zeros((PAD, D), jnp.float32)
        for half in range(2):
            cols = pl.ds(pl.multiple_of(n * 512 + 256 * half, 128), 256)
            pre = nn(x_s[...], up[:, cols])
            cdf = normal_cdf(pre)
            act = to_low(pre * cdf)
            pre_grad = to_low(gelu_slope(pre, cdf) * nn(bg[...], down[:, cols]))
            put_cols(slots[0], cols, nn(x_t[...], pre_grad))
            put_cols(slots[1], cols, nn(bg_t[...], act))
            back = back + nt(pre_grad, up[:, cols])
        din[...] += back

    grad_send(1, t)
    grad_send(2, t)
    yield
    if t == 1:
        back, gain_grad = norm_pull(res[...], gain, din[...])
        stream[...] += back
        put_gain(gain_grad)
        yield


PASS_COUNT = 7
YIELDS = 16
PASS_EVENTS = {
    0: ((0, 0), (1, 0), (2, 0), (3, 0),),
    1: ((0, 1),),
    2: ((1, 1),),
    3: ((2, 1),),
    4: ((3, 1),),
    6: ((0, 2),),
    8: ((1, 2),),
    11: ((2, 2),),
    13: ((0, 3), (3, 2), (1, 3), (2, 3),),
    14: ((0, 4), (3, 3), (1, 4),),
    15: ((0, 5), (3, 4), (1, 5), (2, 4), (0, 6), (3, 5), (1, 6), (2, 5), (4, 0), (3, 6), (5, 0), (2, 6), (4, 1),),
    17: ((6, 0), (5, 1), (4, 2), (6, 1), (5, 2), (4, 3), (6, 2), (5, 3), (4, 4), (6, 3), (5, 4), (4, 5), (6, 4), (5, 5), (4, 6), (6, 5), (5, 6), (6, 6),),
}


def backward_kernel(*refs):
    (act_in, base, stream_in, r1, r2) = refs[:5]
    (qkv0, qkv1, mixed0, mixed1, gain_in, router_in, grad_e, land_e) = refs[5:13]
    (own, landed, late, stream_out, sum_all) = refs[13:18]
    (w, g, stream, res0, x_s, x_t, bg, bg_t, din, dmix, dqkv, rows_s, small_s, tail_s) = refs[18:32]
    w_sem, keep_sem, put_sem, got_sem, small_sem, late_send, late_recv = refs[32:39]
    me = coordinates()
    greet(me)
    sibling = {**me, "c": 1 - me["c"]}
    mine_e = grad_e.at[:, me["c"]]
    passes = [
        (
            mine_e,
            slice(768 * n, 768 * n + 768),
            land_e if n < 2 else late.at[n - 2],
            slice(768 * n, 768 * n + 768) if n < 2 else slice(0, 768),
            sum_all,
            slice(WIDE + 768 * n, WIDE + 768 * n + 768),
        )
        for n in range(4)
    ]
    for a, b in ((1280, 1664), (512, 1280), (0, 512)):
        passes.append((own, slice(a, b), landed, slice(a, b), sum_all, slice(a, b)))
    work = make_reduce(me, passes, refs[39:])

    def late_copy(n, z_lo):
        cols = slice(EARLY + 768 * n, EARLY + 768 * n + 768)
        return remote(
            grad_e.at[z_lo, 1 - me["c"], :, :, :, :, :, cols],
            late.at[n, z_lo],
            late_send.at[n, z_lo],
            late_recv.at[n, z_lo],
            sibling,
        )

    def load_parts(n):
        s, t = BWD_LOADS[n]
        cols = slice(SET_AT[s], SET_AT[s] + CHUNK)
        return [
            pltpu.make_async_copy(
                base.at[q, t, :, cols],
                w.at[n % 3, :, CHUNK * q : CHUNK * q + CHUNK],
                w_sem.at[n, q],
            )
            for q in range(4)
        ]

    def load_start(*numbers):
        for n in numbers:
            for copy in load_parts(n):
                copy.start()

    def load_wait(*numbers):
        for n in numbers:
            for copy in load_parts(n):
                copy.wait()

    work.begin(0)
    load_start(0, 1, 2)
    for n in range(2):
        for z_lo in range(2):
            late_copy(n, z_lo).start()
    work.begin(1)
    work.begin(2)
    work.begin(3)
    small_copy = pltpu.make_async_copy(
        base.at[0, 0, :, pl.ds(SMALL_AT, SMALL)], small_s, small_sem.at[0]
    )
    small_copy.start()
    stream[...] = stream_in[...]
    res0[...] = jnp.zeros((PAD, D), jnp.bfloat16)
    res0[0:SEQ, :] = act_in[...]
    small_copy.wait()
    turned_small = jnp.transpose(small_s[...].astype(jnp.float32))
    gains = [turned_small[j : j + 1, :] for j in range(4)]
    rows_s[...] = jnp.zeros((128, D), jnp.float32)
    rows_s[3:4, :] = gain_in[...]

    def pieces(n):
        s, t = BWD_LOADS[n]
        cols = slice(SET_AT[s], SET_AT[s] + CHUNK)
        copies = []
        for z_lo in range(2):
            at = [
                pl.ds(pl.multiple_of(CHUNK * (2 * z_lo + c), 128), CHUNK)
                for c in (me["c"], 1 - me["c"])
            ]
            keep = pltpu.make_async_copy(
                g.at[n % 2, :, :, :, :, at[0]],
                own.at[z_lo, t, :, :, :, :, cols],
                keep_sem.at[n, z_lo],
            )
            give = remote(
                g.at[n % 2, :, :, :, :, at[1]],
                landed.at[z_lo, t, :, :, :, :, cols],
                put_sem.at[n, z_lo],
                got_sem.at[n, z_lo],
                sibling,
            )
            copies.append((keep, give))
        return copies

    waited = set()

    def send_wait(n):
        if n in waited:
            return
        waited.add(n)
        for keep, give in pieces(n):
            keep.wait()
            give.wait_send()

    def grad_slot(s, t):
        n = BWD_LOADS.index((s, t))
        if n >= 2:
            send_wait(n - 2)
        return g.at[n % 2]

    def grad_send(s, t):
        for keep, give in pieces(BWD_LOADS.index((s, t))):
            keep.start()
            give.start()

    tools = (x_s, x_t, bg, bg_t, din, dmix, dqkv, grad_slot, grad_send)

    def put_gain(j, value):
        rows_s[j : j + 1, :] = value

    def backward():
        load_wait(0, 1)
        yield from attend_backward(
            stream, r2, gains[1], [w.at[0], w.at[1]], qkv1, mixed1, 3, tools,
            functools.partial(put_gain, 1),
        )
        load_start(3, 4)
        load_wait(2, 3)
        put = functools.partial(put_gain, 2)
        yield from dense_backward(stream, r1, gains[2], w.at[2], w.at[0], 0, tools, put)
        load_start(5, 6)
        load_wait(4, 5)
        yield from dense_backward(stream, r1, gains[2], w.at[1], w.at[2], 1, tools, put)
        load_start(7)
        load_wait(6, 7)
        yield from attend_backward(
            stream, res0, gains[0], [w.at[0], w.at[1]], qkv0, mixed0, 0, tools,
            functools.partial(put_gain, 0),
        )

    tails = []
    made_of = {4: (0, 1), 5: (2, 3, 4, 5), 6: (6, 7)}

    def run_events(turn):
        for m, stage in plan.get(turn, ()):
            if stage == 0 and m in (2, 3):
                for z_lo in range(2):
                    late_copy(m - 2, z_lo).wait()
            if stage == 0 and m in made_of:
                for n in made_of[m]:
                    send_wait(n)
                    for _, give in pieces(n):
                        give.wait_recv()
                if m == 6:
                    for keep, give in tails:
                        keep.wait()
                        give.wait()
                work.begin(m)
            work.run(m, stage)

    plan = PASS_EVENTS
    run_events(0)
    for n, _ in enumerate(backward()):
        run_events(n + 1)
    tail_s[...] = to_low(jnp.transpose(rows_s[...]) + router_in[...]).reshape(tail_s.shape)
    for n in range(4):
        place = (n // 2, n % 2, *[slice(None)] * 4, slice(SMALL_AT, SMALL_AT + SMALL))
        keep = pltpu.make_async_copy(tail_s, own.at[place], keep_sem.at[8, n])
        give = remote(tail_s, landed.at[place], put_sem.at[8, n], got_sem.at[8, n], sibling)
        keep.start()
        give.start()
        tails.append((keep, give))
    stream_out[...] = stream[0:SEQ, :]
    run_events(YIELDS + 1)


def run_backward(*args):
    f32, bf16 = jnp.float32, jnp.bfloat16
    shape = jax.ShapeDtypeStruct
    vmem, hbm = pl.BlockSpec(memory_space=pltpu.VMEM), pl.BlockSpec(memory_space=pl.ANY)
    dma = pltpu.SemaphoreType.DMA
    blocks = (2, 2, 2, 4, 2, 48, WIDE)
    cubes = [args[-2].reshape(2, 2, 2, 2, 4, 2, 48, BOTH), args[-1].reshape(2, 2, 2, 4, 2, 48, BOTH)]
    return pl.pallas_call(
        backward_kernel,
        out_shape=[
            shape(blocks, bf16),
            shape(blocks, bf16),
            shape((2, 2, 2, 2, 4, 2, 48, PASS), bf16),
            shape((SEQ, D), f32),
            shape((48, ALL), bf16),
        ],
        in_specs=[vmem, hbm] + [vmem] * 9 + [hbm] * 2,
        out_specs=[hbm, hbm, hbm, vmem, vmem],
        scratch_shapes=[
            pltpu.VMEM((3, D, HALF), bf16),
            pltpu.VMEM((2, 2, 4, 2, 48, HALF), bf16),
            pltpu.VMEM((PAD, D), f32),
            pltpu.VMEM((PAD, D), bf16),
            pltpu.VMEM((PAD, D), bf16),
            pltpu.VMEM((D, PAD), bf16),
            pltpu.VMEM((PAD, D), bf16),
            pltpu.VMEM((D, PAD), bf16),
            pltpu.VMEM((PAD, D), f32),
            pltpu.VMEM((PAD, 384), bf16),
            pltpu.VMEM((PAD, 1152), bf16),
            pltpu.VMEM((128, D), f32),
            pltpu.VMEM((D, 128), bf16),
            pltpu.VMEM((2, 4, 2, 48, 128), bf16),
            dma((8, 4)),
            dma((9, 4)),
            dma((9, 4)),
            dma((9, 4)),
            dma((1,)),
            dma((2, 2)),
            dma((2, 2)),
            *reduce_scratch(PASS_COUNT),
        ],
        compiler_params=pltpu.CompilerParams(
            collective_id=2, has_side_effects=True, vmem_limit_bytes=62 * 1024 * 1024
        ),
        name="backward_reduce",
    )(*args[:-2], *cubes)


def body(
    activations,
    attn_gain,
    qkv_weight,
    out_weight,
    ffn_gain,
    mlp_up,
    mlp_down,
    router,
    expert_up,
    expert_down,
    routes,
    cotangent,
):
    small = jnp.concatenate([attn_gain.T, ffn_gain.T, router], axis=1)
    small = jnp.pad(small, ((0, 0), (0, SMALL - 8)))
    out_t = jnp.transpose(out_weight, (0, 2, 1))
    attn = [jnp.concatenate([qkv_weight[b], out_t[b][None]], axis=0) for b in range(2)]

    def chunks(matrix):
        return jnp.transpose(matrix.reshape(12, 4, CHUNK), (1, 0, 2))

    pair = jnp.stack(
        [
            expert_up.reshape(4, 12, 3, TILE),
            jnp.transpose(expert_down, (0, 2, 1)).reshape(4, 12, 3, TILE),
        ],
        axis=3,
    ).reshape(4, 12, BOTH)
    sets = jnp.concatenate(
        [
            attn[0],
            jnp.broadcast_to(small, (4, *small.shape)),
            chunks(mlp_up),
            chunks(mlp_down.T),
            attn[1],
            pair,
        ],
        axis=2,
    )
    sets = lax.all_to_all(
        sets, "fsdp", split_axis=0, concat_axis=0, tiled=True, axis_index_groups=GROUPS
    )
    shard = sets.reshape(48, ALL)
    half = lax.axis_index("tp")
    my_routes = lax.dynamic_slice_in_dim(routes, half * SEQ, SEQ, 0)
    labels = jnp.arange(-4, 124, dtype=jnp.int32)
    chosen = jnp.sum((my_routes[:, :, None] == labels).astype(jnp.float32), axis=1)
    chosen = jnp.pad(chosen, ((0, PAD - SEQ), (0, 0)))
    outs = run_experts(activations, cotangent, chosen, shard)
    whole, grad_e, land_e, result, stream, r1, r2 = outs[:7]
    qkv0, qkv1, mixed0, mixed1, gain_grad, router_grad = outs[7:]
    _, _, _, stream, sums = run_backward(
        activations, whole.reshape(4, 2, D, ALL), stream, r1, r2, qkv0, qkv1, mixed0, mixed1,
        gain_grad, router_grad, grad_e, land_e,
    )
    sums = sums.reshape(4, 12, ALL)
    sums = lax.all_to_all(
        sums, "fsdp", split_axis=0, concat_axis=0, tiled=True, axis_index_groups=GROUPS
    ).astype(jnp.float32)
    first, up, down, second = [sums[:, :, at : at + CHUNK] for at in SET_AT]
    tail = sums[0, :, SMALL_AT : SMALL_AT + SMALL]
    pair = sums[:, :, WIDE:].reshape(4, 12, 3, 2, TILE)
    return (
        result,
        stream,
        tail[:, 0:2].T,
        jnp.stack([first[:3], second[:3]]),
        jnp.stack([first[3].T, second[3].T]),
        tail[:, 2:4].T,
        jnp.transpose(up, (1, 0, 2)).reshape(12, HALF),
        jnp.transpose(down, (0, 2, 1)).reshape(HALF, 12),
        tail[:, 4:8],
        pair[:, :, :, 0].reshape(4, 12, HALF),
        jnp.transpose(pair[:, :, :, 1].reshape(4, 12, HALF), (0, 2, 1)),
    )


def solution(mesh):
    placed = (
        P(("fsdp", "tp"), None),
        P(None, "fsdp"),
        P(None, None, "fsdp", "tp"),
        P(None, "tp", "fsdp"),
        P(None, "fsdp"),
        P("fsdp", "tp"),
        P("tp", "fsdp"),
        P("fsdp", None),
        P(None, "fsdp", "tp"),
        P(None, "tp", "fsdp"),
        P("fsdp", None),
        P(("fsdp", "tp"), None),
    )
    return jax.shard_map(
        body,
        mesh=mesh,
        in_specs=placed,
        out_specs=(
            P(("fsdp", "tp"), None),
            P(("fsdp", "tp"), None),
            P(None, "fsdp"),
            P(None, None, "fsdp", "tp"),
            P(None, "tp", "fsdp"),
            P(None, "fsdp"),
            P("fsdp", "tp"),
            P("tp", "fsdp"),
            P("fsdp", None),
            P(None, "fsdp", "tp"),
            P(None, "tp", "fsdp"),
        ),
        check_vma=False,
    )
```
